128 devices in a mesh: tm: 8 (over x_hi, y), space: 16 (over z, x_lo, core).
Axes of the slice: x: 4 (x_hi: 2, x_lo: 2; x = x_hi * 2 + x_lo), y: 4, z: 4, core: 2. Of those that a mesh axis runs over, the one named last changes fastest.
Arguments:
- initial: float32 [32, 256, 512], P('space'), may hold values from -6 to 6
- c_values: float32 [16, 32, 256, 512], P('tm', 'space'), may hold values from -6 to 6
- forcing: float32 [32, 256, 512], P('space'), may hold values from -0.6 to 0.6
- classes: int32 [32, 256, 512], P('space'), may hold values from 0 to 7
- diffusion: float32 [8], replicated, may hold values from 0.01 to 0.04
- drift: float32 [3, 8], replicated, may hold values from -1 to 1
Outputs:
- updated: float32 [16, 32, 256, 512], P('tm', 'space')
- residual: float32 [16, 32, 256, 512], P('tm', 'space')
The draws below stay inside these ranges and needn't reach their ends.
All inputs are finite; a program needn't handle non-finite values.
Results may differ from the reference program's by a relative error of at most 0.00002.
Values sent between devices are 32-bit elements; how exact they have to be, the bound alone decides.
No kernel may reach another device: no remote copies, remote signals or barrier semaphores. Data moves between devices by JAX's collectives and lax.ppermute only.
A program may use at most 192 MiB of HBM per device.

```python
import math
import jax
import jax.numpy as jnp
from jax import lax

NY = 256
NX = 512
COARSEN = 4
NCLASS = 8
NZ = 32
NC = 16


def place_ends(array, stream_key, least, top_value):
    shape = array.shape
    index_at = [jax.random.randint(jax.random.fold_in(stream_key, axis), (), 0, shape[axis]) for axis in range(len(shape))]
    array = array.at[tuple(index_at)].set(least)
    longest = shape.index(max(shape))
    index_at[longest] = (index_at[longest] + 1) % shape[longest]
    return array.at[tuple(index_at)].set(top_value)


def level_of(stream_key, shape, cuts, least, high):
    gain = 1.0
    for position, parts in cuts:
        draws = jax.random.uniform(jax.random.fold_in(jax.random.fold_in(stream_key, 6), position), (parts,), jnp.float32, least / len(cuts), high / len(cuts))
        gain = gain * jnp.repeat(jnp.exp(draws), shape[position] // parts).reshape((-1,) + (1,) * (len(shape) - 1 - position))
    return gain


def noise(rng, dims, deviation, bound, split=(), kind=jnp.bfloat16):
    loudness = level_of(rng, dims, split, -0.22, 0.18) if split else 1.0
    entries = jax.random.normal(rng, dims, jnp.float32) * deviation * loudness
    return jnp.minimum(jnp.maximum(entries, -bound), bound).astype(kind)


def setup_inputs(seed: int = 0) -> dict:
    seeds = jax.random.split(jax.random.key(seed), 7)
    initial = noise(seeds[0], (NZ, NY, NX), 1.0, 6.0, ((0, 16),), jnp.float32)
    c_values = noise(seeds[1], (NC, NZ, NY, NX), 1.0, 6.0, ((0, 8), (1, 16)), jnp.float32)
    forcing = noise(seeds[2], (NZ, NY, NX), 0.1, 0.6, ((0, 16),), jnp.float32)
    classes = place_ends(jax.random.randint(seeds[3], (NZ, NY, NX), 0, NCLASS), jax.random.fold_in(seeds[3], 1), 0, NCLASS - 1).astype(jnp.int32)
    diffusion = jnp.clip(jnp.exp(jax.random.uniform(seeds[4], (NCLASS,), jnp.float32, math.log(0.01), math.log(0.04))), 0.01, 0.04)
    drift = jnp.clip(jax.random.uniform(seeds[5], (3, NCLASS), jnp.float32, -1.0, 1.0), -1.0, 1.0)
    return dict(initial=initial, c_values=c_values, forcing=forcing, classes=classes, diffusion=diffusion, drift=drift)


def sweep(padded, a, bz, by, bx, extra):
    centre = padded[..., 1:-1, :, :]
    above = padded[..., 2:, :, :]
    below = padded[..., :-2, :, :]
    total = (1.0 - 6.0 * a) * centre + (a - bz) * above + (a + bz) * below
    total = total + (a - by) * jnp.roll(centre, -1, -2) + (a + by) * jnp.roll(centre, 1, -2)
    total = total + (a - bx) * jnp.roll(centre, -1, -1) + (a + bx) * jnp.roll(centre, 1, -1)
    return total + extra


def wrapped(field):
    return jnp.concatenate([field[-1:], field, field[:1]], axis=0)


def reference(initial, c_values, forcing, classes, diffusion, drift):
    a = diffusion[classes]
    bz = a * drift[0][classes]
    by = a * drift[1][classes]
    bx = a * drift[2][classes]
    scale = jnp.float32(COARSEN)
    ac, bzc, byc, bxc = a * scale, bz * scale, by * scale, bx * scale
    starts = jnp.concatenate([initial[None], c_values[:-1]], axis=0)

    def advance(state):
        for step in range(COARSEN):
            state = sweep(wrapped(state), a, bz, by, bx, forcing)
        return state

    ends = lax.map(advance, starts)
    residual = ends - c_values

    def coarse(error, term):
        error = sweep(wrapped(error), ac, bzc, byc, bxc, term)
        return error, error

    zero = jnp.zeros(initial.shape, jnp.float32)
    unused, errors = lax.scan(coarse, zero, residual)
    return c_values + errors, residual
```

```python
import functools

import jax
import jax.numpy as jnp
import numpy as np
from jax import lax
from jax.experimental import pallas as pl
from jax.experimental.pallas import tpu as pltpu
from jax.sharding import Mesh, PartitionSpec as P

COARSEN = 4
XH, Y, SPACE = 2, 4, 16
NX = 512
XC = NX // 128
ROWS = 4
GROUP = Y * SPACE

POS = []
for s in range(SPACE):
    z, x, core = s >> 2, (s >> 1) & 1, s & 1
    POS.append(2 * (2 * z + (x if z % 2 == 0 else 1 - x)) + core)


def rho(y, s):
    return 4 * POS[s] + (y if POS[s] % 2 == 0 else 3 - y)


BLOCK_OF = [rho(j // SPACE, j % SPACE) for j in range(GROUP)]
DEVICE_AT = [BLOCK_OF.index(p) for p in range(GROUP)]
UP = [(DEVICE_AT[p], DEVICE_AT[(p + 1) % GROUP]) for p in range(GROUP)]
DOWN = [(j, i) for i, j in UP]
TM = ("xh", "y")
RING = ("y", "space")
VMEM = pl.BlockSpec(memory_space=pltpu.VMEM)


def call(kernel, outs, *args, flops=0):
    size = sum(int(np.prod(a.shape)) * 4 for a in args)
    single = not isinstance(outs, (list, tuple))
    out_list = [outs] if single else list(outs)
    size += sum(int(np.prod(o.shape)) * 4 for o in out_list)
    return pl.pallas_call(
        kernel,
        out_shape=outs,
        in_specs=[VMEM] * len(args),
        out_specs=VMEM if single else [VMEM] * len(out_list),
        compiler_params=pltpu.CompilerParams(vmem_limit_bytes=24 << 20),
        cost_estimate=pl.CostEstimate(flops=flops, bytes_accessed=size, transcendentals=0),
    )(*args)


def f32(*shape):
    return jax.ShapeDtypeStruct(shape, jnp.float32)


def pack_kernel(r0, r1, send):
    for j in range(GROUP):
        top = ROWS * BLOCK_OF[j]
        for tt, ref in ((0, r0), (1, r1)):
            for z in range(2):
                for c in range(XC):
                    send[j, tt, c, pl.ds(z, ROWS, stride=2), :] = ref[z, top : top + ROWS, c * 128 : (c + 1) * 128]


def unpack_kernel(recv, r):
    flat = recv.reshape(GROUP * 2 * XC * 8, 128)
    for y in range(Y):
        for tt in range(2):
            for row in range(ROWS):
                for par in range(2):
                    for c in range(XC):
                        first = ((y * SPACE * 2 + tt) * XC + c) * 8 + row * 2 + par
                        r[2 * y + tt, row, par, c] = flat[pl.ds(first, SPACE, stride=2 * XC * 8), :]


def return_pack_kernel(ea, eb, send):
    flat = send.reshape(GROUP * 2 * XC * 8, 128)
    for y in range(Y):
        for tt in range(2):
            for row in range(ROWS):
                for par in range(2):
                    for c in range(XC):
                        k = 2 * y + tt
                        first = ((y * SPACE * 2 + tt) * XC + c) * 8 + row * 2 + par
                        flat[pl.ds(first, SPACE, stride=2 * XC * 8), :] = (ea if k < 4 else eb)[k % 4, row, par, c]


def updated_kernel(recv, c_ref, out):
    for j in range(GROUP):
        top = ROWS * BLOCK_OF[j]
        for tt in range(2):
            for z in range(2):
                for c in range(XC):
                    here = (tt, z, slice(top, top + ROWS), slice(c * 128, (c + 1) * 128))
                    out[here] = c_ref[here] + recv[j, tt, c, pl.ds(z, ROWS, stride=2), :]


def x_shifts(v):
    lane = lax.broadcasted_iota(jnp.int32, v.shape, 2)
    before = pltpu.roll(v, 1, 2)
    after = pltpu.roll(v, 127, 2)
    before = jnp.where(lane == 0, jnp.concatenate([before[-1:], before[:-1]], 0), before)
    after = jnp.where(lane == 127, jnp.concatenate([after[1:], after[:1]], 0), after)
    return before, after


def sweep_row(coef, at, v, up, down, extra):
    result = []
    for p in range(2):
        c = [coef[i, at, p] for i in range(7)]
        if p == 0:
            z_above, z_below = v[1], pltpu.roll(v[1], 1, 1)
        else:
            z_above, z_below = pltpu.roll(v[0], SPACE - 1, 1), v[0]
        before, after = x_shifts(v[p])
        total = c[0] * v[p] + c[1] * z_above + c[2] * z_below
        if up is not None:
            total = total + c[3] * up[p]
        if down is not None:
            total = total + c[4] * down[p]
        total = total + c[5] * after + c[6] * before
        if extra is not None:
            total = total + extra[p]
        result.append(total)
    return result


def pair(ref, *at):
    return [ref[(*at, 0)], ref[(*at, 1)]]


def put(ref, at, value):
    for p in range(2):
        ref[(*at, p)] = value[p]


HALO = 2


def trajectory(coef, r, first, width, start, low, high):
    rows = start
    for j in range(width):
        put(low, (j,), rows[0])
        put(high, (j,), rows[-1])
        if j + 1 < width:
            rows = [
                sweep_row(
                    coef, HALO + i, rows[i], rows[i + 1] if i + 1 < ROWS else None, rows[i - 1] if i else None,
                    pair(r, first + j, i),
                )
                for i in range(ROWS)
            ]


def advance(coef, r, first, width, start, below, above, store):
    rows = start
    dev_low, dev_high = {}, {}
    for j in range(width):
        under, over = pair(below, j), pair(above, j)
        if 1 in dev_low:
            under = [a + b for a, b in zip(under, dev_low[1])]
            over = [a + b for a, b in zip(over, dev_high[1])]
        padded = [under] + rows + [over]
        new_low, new_high = {}, {}
        for i in range(1, min(j + 1, width - j - 1) + 1):
            if i <= j:
                new_low[i] = sweep_row(coef, HALO - i, dev_low[i], rows[0] if i == 1 else dev_low[i - 1], dev_low.get(i + 1), None)
                new_high[i] = sweep_row(
                    coef, HALO + ROWS - 1 + i, dev_high[i], dev_high.get(i + 1), rows[-1] if i == 1 else dev_high[i - 1], None
                )
            else:
                source_low = rows[0] if i == 1 else dev_low[i - 1]
                source_high = rows[-1] if i == 1 else dev_high[i - 1]
                new_low[i] = [coef[3, HALO - i, p] * source_low[p] for p in range(2)]
                new_high[i] = [coef[4, HALO + ROWS - 1 + i, p] * source_high[p] for p in range(2)]
        rows = [
            sweep_row(coef, HALO + i, padded[i + 1], padded[i + 2], padded[i], pair(r, first + j, i)) for i in range(ROWS)
        ]
        dev_low, dev_high = new_low, new_high
        if store is not None:
            for i in range(ROWS):
                put(store, (j, i), rows[i])
    return rows


def start_kernel(first, width, coef, r, start, low, high):
    trajectory(coef, r, first, width, [pair(start, i) for i in range(ROWS)], low, high)


def middle_kernel(first, width, then, coef, r, start, below, above, errors, low, high):
    rows = advance(coef, r, first, width, [pair(start, i) for i in range(ROWS)], below, above, errors)
    trajectory(coef, r, first + width, then, rows, low, high)


def end_kernel(first, width, coef, r, start, below, above, errors):
    advance(coef, r, first, width, [pair(start, i) for i in range(ROWS)], below, above, errors)


def exchange(low, high):
    return lax.ppermute(high, RING, UP), lax.ppermute(low, RING, DOWN)


def coarse(coef, r, start, first, widths):
    row = (2, XC, SPACE, 128)
    a, b = widths
    low, high = call(functools.partial(start_kernel, first, a), [f32(a, *row)] * 2, coef, r, start, flops=1 << 24)
    below, above = exchange(low, high)
    early, low, high = call(
        functools.partial(middle_kernel, first, a, b), [f32(a, ROWS, *row)] + [f32(b, *row)] * 2,
        coef, r, start, below, above, flops=1 << 25,
    )
    below, above = exchange(low, high)
    late = call(functools.partial(end_kernel, first + a, b), f32(b, ROWS, *row), coef, r, early[a - 1], below, above, flops=1 << 24)
    return early, late


def fine_sweep(v, below, above, c, extra):
    up = jnp.concatenate([v[1:], above], axis=0)
    down = jnp.concatenate([below, v[:-1]], axis=0)
    total = c[0] * v + c[1] * up + c[2] * down
    total = total + c[3] * jnp.roll(v, -1, -2) + c[4] * jnp.roll(v, 1, -2)
    total = total + c[5] * jnp.roll(v, -1, -1) + c[6] * jnp.roll(v, 1, -1)
    return total + extra


def coefficients(classes, diffusion, drift, scale):
    a = diffusion * 1.0
    bz, by, bx = a * drift[0], a * drift[1], a * drift[2]
    a, bz, by, bx = a * scale, bz * scale, by * scale, bx * scale
    tables = [1.0 - 6.0 * a, a - bz, a + bz, a - by, a + by, a - bx, a + bx]
    fields = [jnp.zeros(classes.shape, jnp.float32)] * 7
    for label in range(diffusion.shape[0]):
        picked = classes == label
        fields = [jnp.where(picked, table[label], field) for table, field in zip(tables, fields)]
    return fields


def block_classes(classes, y):
    parts = classes.reshape(2, SPACE, 4, ROWS, NX)
    even = lax.dynamic_index_in_dim(parts, y, axis=2, keepdims=False)
    odd = lax.dynamic_index_in_dim(parts, 3 - y, axis=2, keepdims=False)
    mine = jnp.stack([(even if POS[s] % 2 == 0 else odd)[:, POS[s]] for s in range(SPACE)])
    got = lax.all_to_all(mine, "space", 0, 0, tiled=True)
    got = got.reshape(SPACE, 2, ROWS, XC, 128).transpose(2, 1, 3, 0, 4)
    below = lax.ppermute(got[ROWS - HALO :], RING, UP)
    above = lax.ppermute(got[:HALO], RING, DOWN)
    return jnp.concatenate([below, got, above], axis=0)


def shards(initial, c_values, forcing, classes, diffusion, drift):
    t = lax.axis_index(TM)
    xh, y = lax.axis_index("xh"), lax.axis_index("y")
    ring_up = [(i, (i + 1) % SPACE) for i in range(SPACE)]
    ring_down = [(j, i) for i, j in ring_up]
    previous = lax.ppermute(c_values[1], TM, [(i, i + 1) for i in range(XH * Y - 1)])
    fine = coefficients(classes, diffusion, drift, jnp.float32(1.0))
    states = [jnp.where(t == 0, initial, previous), c_values[0]]
    for step in range(COARSEN):
        for slot in (1, 0):
            v = states[slot]
            below = lax.ppermute(v[1:], "space", ring_up)
            above = lax.ppermute(v[:1], "space", ring_down)
            states[slot] = fine_sweep(v, below, above, fine, forcing)
    r0, r1 = states[0] - c_values[0], states[1] - c_values[1]
    residual = jnp.stack([r0, r1])

    coef = jnp.stack(coefficients(block_classes(classes, y), diffusion, drift, jnp.float32(COARSEN)))
    send = call(pack_kernel, f32(GROUP, 2, XC, 8, 128), r0, r1)
    recv = lax.all_to_all(send, RING, 0, 0, tiled=True)
    r = call(unpack_kernel, f32(2 * Y, ROWS, 2, XC, SPACE, 128), recv)

    early, late = coarse(coef, r, r[0], 1, (4, 3))
    carried = lax.ppermute(late[2], "xh", [(0, 1)])
    early, late = coarse(coef, r, carried, 0, (4, 4))
    back = call(return_pack_kernel, f32(GROUP, 2, XC, 8, 128), early, late)
    got = lax.all_to_all(back, RING, 0, 0, tiled=True)
    updated = call(updated_kernel, f32(*c_values.shape), got, c_values)
    return updated, residual


def solution(mesh):
    split = Mesh(np.asarray(mesh.devices).reshape(XH, Y, SPACE), ("xh", "y", "space"))
    return jax.shard_map(
        shards,
        mesh=split,
        in_specs=(P("space"), P(TM, "space"), P("space"), P("space"), P(), P()),
        out_specs=(P(TM, "space"), P(TM, "space")),
        check_vma=False,
    )
```

```python
import functools

import jax
import jax.numpy as jnp
import numpy as np
from jax import lax
from jax.experimental import pallas as pl
from jax.experimental.pallas import tpu as pltpu
from jax.sharding import Mesh, PartitionSpec as P

COARSEN = 4
XH, Y, SPACE = 2, 4, 16
XC = 4
ROWS = 4
HALO = 3
GROUP = Y * SPACE
TIMES = 2 * Y
ROW = (2, XC, SPACE, 128)


def rho(y, s):
    z, x, core = s >> 2, (s >> 1) & 1, s & 1
    chip = 4 * z + (y if z % 2 == 0 else 3 - y)
    return 2 * (chip if x == 0 else 31 - chip) + core


BLOCK_OF = [rho(j // SPACE, j % SPACE) for j in range(GROUP)]
DEVICE_AT = [BLOCK_OF.index(p) for p in range(GROUP)]
UP = [(DEVICE_AT[p], DEVICE_AT[(p + 1) % GROUP]) for p in range(GROUP)]
DOWN = [(j, i) for i, j in UP]
TM = ("xh", "y")
RING = ("y", "space")
VMEM = pl.BlockSpec(memory_space=pltpu.VMEM)
SMEM = pl.BlockSpec(memory_space=pltpu.SMEM)


def f32(*shape):
    return jax.ShapeDtypeStruct(shape, jnp.float32)


def call(kernel, outs, *args, flops=0, scalars=0):
    single = not isinstance(outs, (list, tuple))
    out_list = [outs] if single else list(outs)
    size = sum(int(np.prod(a.shape)) * 4 for a in list(args) + out_list)
    return pl.pallas_call(
        kernel,
        out_shape=outs,
        in_specs=[SMEM] * scalars + [VMEM] * (len(args) - scalars),
        out_specs=VMEM if single else [VMEM] * len(out_list),
        compiler_params=pltpu.CompilerParams(vmem_limit_bytes=24 << 20),
        cost_estimate=pl.CostEstimate(flops=flops, bytes_accessed=size, transcendentals=0),
    )(*args)


def lanes(c):
    return slice(c * 128, (c + 1) * 128)


def pack_kernel(field, send):
    for j in range(GROUP):
        top = ROWS * BLOCK_OF[j]
        for tt in range(2):
            for z in range(2):
                for c in range(XC):
                    send[j, tt, c, pl.ds(z, ROWS, stride=2), :] = field[tt, z, top : top + ROWS, lanes(c)]


def pack_shared_kernel(y_ref, initial, forcing, classes, send):
    for y in range(Y):

        @pl.when(y_ref[0] == y)
        def _():
            for s in range(SPACE):
                top = ROWS * rho(y, s)
                for n, ref in enumerate((initial, forcing, classes)):
                    for z in range(2):
                        for c in range(XC):
                            send[s, n, c, pl.ds(z, ROWS, stride=2), :] = ref[z, top : top + ROWS, lanes(c)].astype(jnp.float32)


def unpack_shared_kernel(recv, initial, forcing, classes, low, high):
    flat = recv.reshape(SPACE * 3 * XC * 8, 128)
    for row in range(ROWS):
        for par in range(2):
            for c in range(XC):
                for n, ref in enumerate((initial, forcing, classes)):
                    part = flat[pl.ds((n * XC + c) * 8 + row * 2 + par, SPACE, stride=3 * XC * 8), :]
                    ref[row, par, c] = part
                    if n > 0 and row < HALO:
                        low[n - 1, row, par, c] = part
                    if n > 0 and row >= ROWS - HALO:
                        high[n - 1, row - ROWS + HALO, par, c] = part


def unpack_kernel(recv, own, early, late, last):
    flat = recv.reshape(GROUP * 2 * XC * 8, 128)
    for y in range(Y):
        for tt in range(2):
            k = 2 * y + tt
            copy, at = (early, k) if k < 3 else (late, k - 3) if k < 7 else (last, 0)
            for row in range(ROWS):
                for par in range(2):
                    for c in range(XC):
                        first = ((y * SPACE * 2 + tt) * XC + c) * 8 + row * 2 + par
                        part = flat[pl.ds(first, SPACE, stride=2 * XC * 8), :]
                        own[k, row, par, c] = part
                        copy[at, row, par, c] = part


def return_pack_kernel(early, late, send):
    flat = send.reshape(GROUP * 2 * XC * 8, 128)
    for y in range(Y):
        for tt in range(2):
            k = 2 * y + tt
            for row in range(ROWS):
                for par in range(2):
                    for c in range(XC):
                        first = ((y * SPACE * 2 + tt) * XC + c) * 8 + row * 2 + par
                        flat[pl.ds(first, SPACE, stride=2 * XC * 8), :] = (early if k < 4 else late)[k % 4, row, par, c]


def return_kernel(recv, *refs):
    out = refs[-1]
    for j in range(GROUP):
        top = ROWS * BLOCK_OF[j]
        for tt in range(2):
            for z in range(2):
                for c in range(XC):
                    here = (tt, z, slice(top, top + ROWS), lanes(c))
                    part = recv[j, tt, c, pl.ds(z, ROWS, stride=2), :]
                    out[here] = part if len(refs) == 1 else refs[0][here] + part


def coefficient_kernel(tables, own, below, above, coef):
    for i in range(ROWS + 2 * HALO):
        ref, n, at = (below, 1, i) if i < HALO else (above, 1, i - HALO - ROWS) if i >= HALO + ROWS else (own, None, i - HALO)
        for par in range(2):
            for c in range(XC):
                piece = ref[at, par, c] if n is None else ref[n, at, par, c]
                label = piece.astype(jnp.int32)
                for t in range(8):
                    table = jnp.broadcast_to(tables[t : t + 1, :], label.shape)
                    coef[t, i, par, c] = jnp.take_along_axis(table, label, axis=1, mode="promise_in_bounds")


def x_shifts(v):
    lane = lax.broadcasted_iota(jnp.int32, v.shape, 2)
    before = pltpu.roll(v, 1, 2)
    after = pltpu.roll(v, 127, 2)
    before = jnp.where(lane == 0, jnp.concatenate([before[-1:], before[:-1]], 0), before)
    after = jnp.where(lane == 127, jnp.concatenate([after[1:], after[:1]], 0), after)
    return before, after


def sweep_row(coef, row, v, up, down, extra, coarse):
    at = HALO + row
    result = []
    for p in range(2):
        if p == 0:
            z_above, z_below = v[1], pltpu.roll(v[1], 1, 1)
        else:
            z_above, z_below = pltpu.roll(v[0], SPACE - 1, 1), v[0]
        before, after = x_shifts(v[p])
        total = coef[1, at, p] * z_above + coef[2, at, p] * z_below
        if up is not None:
            total = total + coef[3, at, p] * up[p]
        if down is not None:
            total = total + coef[4, at, p] * down[p]
        total = total + coef[5, at, p] * after + coef[6, at, p] * before
        if coarse:
            total = coef[7, at, p] * v[p] + COARSEN * total
        else:
            total = coef[0, at, p] * v[p] + total
        if extra is not None:
            total = total + extra[p]
        result.append(total)
    return result


def pair(ref, *at):
    return [ref[(*at, 0)], ref[(*at, 1)]]


def put(ref, at, value):
    for p in range(2):
        ref[(*at, p)] = value[p]


def fine_time(coef, force, own, below, above, target, out):
    rows = {i: pair(*own, i) for i in range(ROWS)}
    rows |= {i - ROWS: pair(*below, i) for i in range(ROWS)}
    rows |= {i + ROWS: pair(*above, i) for i in range(ROWS)}
    for step in range(COARSEN):
        reach = COARSEN - 1 - step
        rows = {
            i: sweep_row(coef, i, rows[i], rows[i + 1], rows[i - 1], force(i), False) for i in range(-reach, ROWS + reach)
        }
    for i in range(ROWS):
        goal = pair(*target, i)
        put(out[0], (*out[1:], i), [rows[i][p] - goal[p] for p in range(2)])


def forcing_rows(own, below, above):
    def at(i):
        return pair(below, 0, i + HALO) if i < 0 else pair(above, 0, i - ROWS) if i >= ROWS else pair(own, i)

    return at


def fine_early_kernel(coef, f, f_below, f_above, start, own, start_below, start_above, below, above, out):
    force = forcing_rows(f, f_below, f_above)
    fine_time(coef, force, (start,), (start_below,), (start_above,), (own, 0), (out, 0))

    @pl.loop(1, 4)
    def _(k):
        fine_time(coef, force, (own, k - 1), (below, k - 1), (above, k - 1), (own, k), (out, k))


def fine_late_kernel(coef, f, f_below, f_above, own, below, above, out):
    force = forcing_rows(f, f_below, f_above)

    @pl.loop(0, 4)
    def _(k):
        fine_time(coef, force, (own, k + 3), (below, k), (above, k), (own, k + 4), (out, k))


def trajectory(coef, r, first, width, start, low, high):
    rows = start
    for j in range(width):
        put(low, (j,), rows[0])
        put(high, (j,), rows[-1])
        if j + 1 < width:
            rows = [
                sweep_row(
                    coef, i, rows[i], rows[i + 1] if i + 1 < ROWS else None, rows[i - 1] if i else None,
                    pair(r, first + j, i), True,
                )
                for i in range(ROWS)
            ]


def advance(coef, r, first, width, start, below, above, store):
    rows = start
    dev_low, dev_high = {}, {}
    for j in range(width):
        under, over = pair(below, j), pair(above, j)
        if 1 in dev_low:
            under = [a + b for a, b in zip(under, dev_low[1])]
            over = [a + b for a, b in zip(over, dev_high[1])]
        padded = [under] + rows + [over]
        new_low, new_high = {}, {}
        for i in range(1, min(j + 1, width - j - 1) + 1):
            source_low = rows[0] if i == 1 else dev_low[i - 1]
            source_high = rows[-1] if i == 1 else dev_high[i - 1]
            if i <= j:
                new_low[i] = sweep_row(coef, -i, dev_low[i], source_low, dev_low.get(i + 1), None, True)
                new_high[i] = sweep_row(coef, ROWS - 1 + i, dev_high[i], dev_high.get(i + 1), source_high, None, True)
            else:
                new_low[i] = [COARSEN * coef[3, HALO - i, p] * source_low[p] for p in range(2)]
                new_high[i] = [COARSEN * coef[4, HALO + ROWS - 1 + i, p] * source_high[p] for p in range(2)]
        rows = [sweep_row(coef, i, padded[i + 1], padded[i + 2], padded[i], pair(r, first + j, i), True) for i in range(ROWS)]
        dev_low, dev_high = new_low, new_high
        for i in range(ROWS):
            put(store, (j, i), rows[i])
    return rows


def block(ref, *at):
    return [pair(ref, *at, i) for i in range(ROWS)]


def start_kernel(first, width, coef, r, start, low, high):
    trajectory(coef, r, first, width, block(start), low, high)


def middle_kernel(first, width, then, coef, r, r_next, start, below, above, errors, low, high):
    rows = advance(coef, r, first, width, block(start), below, above, errors)
    trajectory(coef, r_next, 0, then, rows, low, high)


def end_kernel(width, coef, r, start, below, above, errors):
    advance(coef, r, 0, width, block(start), below, above, errors)


def exchange(low, high):
    return lax.ppermute(high, RING, UP), lax.ppermute(low, RING, DOWN)


def coarse(coef, r_early, r_late, start, first):
    a, b = 4 - first, 4
    low, high = call(functools.partial(start_kernel, first, a), [f32(a, *ROW)] * 2, coef, r_early, start, flops=1 << 24)
    below, above = exchange(low, high)
    early, low, high = call(
        functools.partial(middle_kernel, first, a, b), [f32(a, ROWS, *ROW)] + [f32(b, *ROW)] * 2,
        coef, r_early, r_late, start, below, above, flops=1 << 25,
    )
    below, above = exchange(low, high)
    late = call(functools.partial(end_kernel, b), f32(b, ROWS, *ROW), coef, r_late, early[a - 1], below, above, flops=1 << 24)
    return early, late


def class_tables(diffusion, drift):
    a = diffusion
    bz, by, bx = a * drift[0], a * drift[1], a * drift[2]
    scale = jnp.float32(COARSEN)
    tables = jnp.stack([1.0 - 6.0 * a, a - bz, a + bz, a - by, a + by, a - bx, a + bx, 1.0 - 6.0 * (a * scale)])
    return jnp.pad(tables, ((0, 0), (0, 128 - tables.shape[1])))


def shards(initial, c_values, forcing, classes, diffusion, drift):
    xh, y = lax.axis_index("xh"), lax.axis_index("y")
    parcel = (2, XC, 8, 128)

    shared = call(pack_shared_kernel, f32(SPACE, 3, XC, 8, 128), y.reshape(1), initial, forcing, classes, scalars=1)
    shared = lax.all_to_all(shared, "space", 0, 0, tiled=True)
    send = call(pack_kernel, f32(GROUP, *parcel), c_values)
    recv = lax.all_to_all(send, RING, 0, 0, tiled=True)

    start, f, label, low, high = call(
        unpack_shared_kernel, [f32(ROWS, *ROW)] * 3 + [f32(2, HALO, *ROW)] * 2, shared
    )
    f_below, f_above = exchange(low, high)
    coef = call(coefficient_kernel, f32(8, ROWS + 2 * HALO, *ROW), class_tables(diffusion, drift), label, f_below, f_above)

    own, c_early, c_late, c_last = call(
        unpack_kernel, [f32(TIMES, ROWS, *ROW), f32(3, ROWS, *ROW), f32(4, ROWS, *ROW), f32(1, ROWS, *ROW)], recv
    )
    before = lax.ppermute(c_last, "xh", [(0, 1)])
    below_early, above_early = exchange(c_early, c_early)
    start = jnp.where(xh == 0, start, before[0])
    start_below, start_above = exchange(start, start)
    below_late, above_late = exchange(c_late, c_late)
    r_early = call(
        fine_early_kernel, f32(4, ROWS, *ROW),
        coef, f, f_below, f_above, start, own, start_below, start_above, below_early, above_early, flops=1 << 27,
    )
    r_late = call(
        fine_late_kernel, f32(4, ROWS, *ROW), coef, f, f_below, f_above, own, below_late, above_late, flops=1 << 27
    )

    early, late = coarse(coef, r_early, r_late, r_early[0], 1)
    carried = lax.ppermute(late[3], "xh", [(0, 1)])
    back = call(return_pack_kernel, f32(GROUP, *parcel), r_early, r_late)
    got = lax.all_to_all(back, RING, 0, 0, tiled=True)
    residual = call(return_kernel, f32(*c_values.shape), got)

    early, late = coarse(coef, r_early, r_late, carried, 0)
    back = call(return_pack_kernel, f32(GROUP, *parcel), early, late)
    got = lax.all_to_all(back, RING, 0, 0, tiled=True)
    updated = call(return_kernel, f32(*c_values.shape), got, c_values)
    return updated, residual


def solution(mesh):
    split = Mesh(np.asarray(mesh.devices).reshape(XH, Y, SPACE), ("xh", "y", "space"))
    return jax.shard_map(
        shards,
        mesh=split,
        in_specs=(P("space"), P(TM, "space"), P("space"), P("space"), P(), P()),
        out_specs=(P(TM, "space"), P(TM, "space")),
        check_vma=False,
    )
```

```python
import functools

import jax
import jax.numpy as jnp
import numpy as np
from jax import lax
from jax.experimental import pallas as pl
from jax.experimental.pallas import tpu as pltpu
from jax.sharding import Mesh, PartitionSpec as P

COARSEN = 4
XH, Y, SPACE = 2, 4, 16
XC = 4
ROWS = 4
HALO = 3
GROUP = Y * SPACE
TIMES = 2 * Y
ROW = (2, XC, SPACE, 128)


def rho(y, s):
    z, x, core = s >> 2, (s >> 1) & 1, s & 1
    chip = 4 * z + (y if z % 2 == 0 else 3 - y)
    return 2 * (chip if x == 0 else 31 - chip) + core


BLOCK_OF = [rho(j // SPACE, j % SPACE) for j in range(GROUP)]
DEVICE_AT = [BLOCK_OF.index(p) for p in range(GROUP)]
RING = ("y", "space")
ALL = ("xh", "y", "space")
UP = [(DEVICE_AT[p], DEVICE_AT[(p + 1) % GROUP]) for p in range(GROUP)]
UP += [(GROUP + (i ^ 2), GROUP + (j ^ 2)) for i, j in UP]
DOWN = [(j, i) for i, j in UP]
ACROSS = [(j, GROUP + (j ^ 2)) for j in range(GROUP)]
TM = ("xh", "y")
VMEM = pl.BlockSpec(memory_space=pltpu.VMEM)
SMEM = pl.BlockSpec(memory_space=pltpu.SMEM)


def f32(*shape):
    return jax.ShapeDtypeStruct(shape, jnp.float32)


def call(kernel, outs, *args, flops=0, scalars=0):
    single = not isinstance(outs, (list, tuple))
    out_list = [outs] if single else list(outs)
    size = sum(int(np.prod(a.shape)) * 4 for a in list(args) + out_list)
    return pl.pallas_call(
        kernel,
        out_shape=outs,
        in_specs=[SMEM] * scalars + [VMEM] * (len(args) - scalars),
        out_specs=VMEM if single else [VMEM] * len(out_list),
        compiler_params=pltpu.CompilerParams(vmem_limit_bytes=16 << 20),
        cost_estimate=pl.CostEstimate(flops=flops, bytes_accessed=size, transcendentals=0),
    )(*args)


def lanes(c):
    return slice(c * 128, (c + 1) * 128)


PARCEL = 2 * XC + 3


def mirrored(xh, j):
    return jnp.where(xh == 0, j, j ^ 2)


def pack_kernel(at_ref, *refs):
    inputs, send, held, done = refs[:4], refs[4], refs[5:9], refs[9]
    planes = [(0, (tt, z)) for z in range(2) for tt in range(2)] + [(n, (z,)) for z in range(2) for n in range(1, 4)]
    copies = [pltpu.make_async_copy(inputs[n].at[i], held[n].at[i], done.at[m]) for m, (n, i) in enumerate(planes)]
    for copy in copies:
        copy.start()
    mine = pl.ds(pl.multiple_of(at_ref[1] * 128, 128), 128)
    for copy, (n, i) in zip(copies, planes):
        copy.wait()
        spread = pl.ds(i[-1], ROWS, stride=2)
        for j in range(GROUP):
            rows = slice(ROWS * BLOCK_OF[j], ROWS * BLOCK_OF[j] + ROWS)
            to = mirrored(at_ref[0], j)
            if n == 0:
                for c in range(XC):
                    send[to, i[0] * XC + c, spread, :] = held[0][(*i, rows, lanes(c))]
            else:
                send[to, 2 * XC + n - 1, spread, :] = held[n][(*i, rows, mine)].astype(jnp.float32)


EARLY, LATE = 5, 4
EDGE = EARLY * ROWS


def unpack_kernel(recv, up, down, second, label, force):
    flat = recv.reshape(GROUP * PARCEL * 8, 128)

    def piece(y, n, row, par):
        return flat[pl.ds((y * SPACE * PARCEL + n) * 8 + row * 2 + par, SPACE, stride=PARCEL * 8), :]

    for y in range(Y):
        for row in range(ROWS):
            for par in range(2):
                for tt in range(2):
                    k = 2 * y + tt
                    for c in range(XC):
                        part = piece(y, tt * XC + c, row, par)
                        if k < EARLY - 1:
                            up[(k + 1) * ROWS + row, par, c] = part
                            down[(k + 1) * ROWS + row, par, c] = part
                        else:
                            second[k - EARLY + 1, row, par, c] = part
                part = piece(y, 2 * XC, row, par)
                up[row, par, y] = part
                down[row, par, y] = part
                for n, ref in enumerate((force, label)):
                    part = piece(y, 2 * XC + 1 + n, row, par)
                    ref[row, par, y] = part
                    first = EDGE + (1 - n) * HALO
                    if row < HALO:
                        down[first + row, par, y] = part
                    if row >= ROWS - HALO:
                        up[first + row - ROWS + HALO, par, y] = part


def return_pack_kernel(early, late, first, r_early, r_late, send):
    flat = send.reshape(GROUP * 4 * XC * 8, 128)
    r = residual_rows(first, r_early, r_late)
    for y in range(Y):
        for tt in range(2):
            k = 2 * y + tt
            for row in range(ROWS):
                for n, rows in enumerate((pair((early, late)[k // 4], k % 4, row), r(k, row))):
                    for par in range(2):
                        for c in range(XC):
                            at = ((y * SPACE * 2 + n) * 2 + tt) * XC + c
                            flat[pl.ds(at * 8 + row * 2 + par, SPACE, stride=4 * XC * 8), :] = rows[par][c]


def return_kernel(at_ref, recv, field, updated, residual, new, rest, done):
    copies = []
    for tt in range(2):
        for z in range(2):
            spread = pl.ds(z, ROWS, stride=2)
            for n in range(GROUP):
                rows = slice(ROWS * BLOCK_OF[n], ROWS * BLOCK_OF[n] + ROWS)
                j = mirrored(at_ref[0], n)
                for c in range(XC):
                    here = (tt, z, rows, lanes(c))
                    new[here] = field[here] + recv[j, tt * XC + c, spread, :]
                    rest[here] = recv[j, (2 + tt) * XC + c, spread, :]
            for held, out in ((new, updated), (rest, residual)):
                copies.append(pltpu.make_async_copy(held.at[tt, z], out.at[tt, z], done.at[len(copies)]))
                copies[-1].start()
    for copy in copies:
        copy.wait()


def fill_coefficients(diffusion, drift, label, below, above, coef):
    lane = lax.broadcasted_iota(jnp.int32, (SPACE, 128), 1)
    tables = [jnp.zeros((SPACE, 128), jnp.float32)] * 8
    for n in range(diffusion.shape[0]):
        a = diffusion[n]
        bz, by, bx = a * drift[0, n], a * drift[1, n], a * drift[2, n]
        values = [1.0 - 6.0 * a, a - bz, a + bz, a - by, a + by, a - bx, a + bx, 1.0 - 6.0 * (a * COARSEN)]
        tables = [jnp.where(lane == n, value, table) for value, table in zip(values, tables)]
    for i in range(-HALO, ROWS + HALO):
        ref, at = (below, EDGE + HALO + i) if i < 0 else (above, EDGE + i - ROWS) if i >= ROWS else (label, i)
        for par in range(2):
            for c in range(XC):
                index = ref[at, par, c].astype(jnp.int32)
                for t in range(8):
                    coef[t, HALO + i, par, c] = jnp.take_along_axis(tables[t], index, axis=1, mode="promise_in_bounds")


def x_shifts(v):
    lane = lax.broadcasted_iota(jnp.int32, v.shape, 2)
    before = pltpu.roll(v, 1, 2)
    after = pltpu.roll(v, 127, 2)
    before = jnp.where(lane == 0, jnp.concatenate([before[-1:], before[:-1]], 0), before)
    after = jnp.where(lane == 127, jnp.concatenate([after[1:], after[:1]], 0), after)
    return before, after


def sweep_row(coef, row, v, up, down, extra, coarse):
    at = HALO + row
    result = []
    for p in range(2):
        if p == 0:
            z_above, z_below = v[1], pltpu.roll(v[1], 1, 1)
        else:
            z_above, z_below = pltpu.roll(v[0], SPACE - 1, 1), v[0]
        before, after = x_shifts(v[p])
        total = coef[1, at, p] * z_above + coef[2, at, p] * z_below
        if up is not None:
            total = total + coef[3, at, p] * up[p]
        if down is not None:
            total = total + coef[4, at, p] * down[p]
        total = total + coef[5, at, p] * after + coef[6, at, p] * before
        if coarse:
            total = coef[7, at, p] * v[p] + COARSEN * total
        else:
            total = coef[0, at, p] * v[p] + total
        if extra is not None:
            total = total + extra[p]
        result.append(total)
    return result


def pair(ref, *at):
    return [ref[(*at, 0)], ref[(*at, 1)]]


def put(ref, at, value):
    for p in range(2):
        ref[(*at, p)] = value[p]


def fine_times(coef, force, starts):
    all_rows = []
    for own, below, above in starts:
        rows = {i: own(i) for i in range(ROWS)}
        rows |= {i - ROWS: below(i) for i in range(ROWS)}
        rows |= {i + ROWS: above(i) for i in range(ROWS)}
        all_rows.append(rows)
    for step in range(COARSEN):
        reach = COARSEN - 1 - step
        new = [{} for _ in starts]
        for i in range(-reach, ROWS + reach):
            for rows, out in zip(all_rows, new):
                out[i] = sweep_row(coef, i, rows[i], rows[i + 1], rows[i - 1], force(i), False)
        all_rows = new
    return [[rows[i] for i in range(ROWS)] for rows in all_rows]


def forcing_rows(own, below, above):
    first = EDGE + HALO

    def at(i):
        return pair(below, first + HALO + i) if i < 0 else pair(above, first + i - ROWS) if i >= ROWS else pair(own, i)

    return at


def minus(a, b):
    return [x - y for x, y in zip(a, b)]


def fine_early_kernel(diffusion, drift, label, force, up, below, above, second, coef, r, first):
    fill_coefficients(diffusion, drift, label, below, above, coef)
    extra = forcing_rows(force, below, above)

    def results(*times):
        return fine_times(coef, extra, [[lambda i, ref=ref, k=k: pair(ref, k * ROWS + i) for ref in (up, below, above)] for k in times])

    @pl.loop(0, EARLY // 2)
    def _(n):
        for k, rows in zip((2 * n, 2 * n + 1), results(2 * n, 2 * n + 1)):
            for i in range(ROWS):
                put(r, (k, i), minus(rows[i], pair(up, (k + 1) * ROWS + i)))

    for i in range(ROWS):
        put(first, (i,), pair(r, 0, i))
    (rows,) = results(EARLY - 1)
    for i in range(ROWS):
        put(r, (EARLY - 1, i), minus(rows[i], pair(second, 0, i)))


def fine_late_kernel(coef, force, edge_below, edge_above, second, below, above, order, r, beyond):
    extra = forcing_rows(force, edge_below, edge_above)

    def results(*times):
        return fine_times(coef, extra, [[lambda i, ref=ref, k=k: pair(ref, k, i) for ref in (second, below, above)] for k in times])

    @pl.loop(0, LATE // 2)
    def _(n):
        even, odd = results(2 * n, 2 * n + 1)
        for i in range(ROWS):
            put(r, (2 * n, i), minus(even[i], pair(second, 2 * n + 1, i)))

            @pl.when(n == 0)
            def _():
                put(r, (1, i), minus(odd[i], pair(second, 2, i)))

            @pl.when(n == 1)
            def _():
                put(beyond, (i,), odd[i])


def residual_rows(first, early, late):
    def at(k, i):
        return pair(first, i) if k == 0 else pair(early, k, i) if k < EARLY else pair(late, k - EARLY, i)

    return at


def trajectory(coef, r, first, width, start, low, high):
    rows = start
    for j in range(width):
        put(low, (j,), rows[0])
        put(high, (j,), rows[-1])
        if j + 1 < width:
            rows = [
                sweep_row(
                    coef, i, rows[i], rows[i + 1] if i + 1 < ROWS else None, rows[i - 1] if i else None,
                    r(first + j, i), True,
                )
                for i in range(ROWS)
            ]


def advance(coef, r, first, width, start, below, above, store):
    rows = start
    dev_low, dev_high = {}, {}
    for j in range(width):
        under, over = pair(below, j), pair(above, j)
        if 1 in dev_low:
            under = [a + b for a, b in zip(under, dev_low[1])]
            over = [a + b for a, b in zip(over, dev_high[1])]
        padded = [under] + rows + [over]
        new_low, new_high = {}, {}
        for i in range(1, min(j + 1, width - j - 1) + 1):
            source_low = rows[0] if i == 1 else dev_low[i - 1]
            source_high = rows[-1] if i == 1 else dev_high[i - 1]
            if i <= j:
                new_low[i] = sweep_row(coef, -i, dev_low[i], source_low, dev_low.get(i + 1), None, True)
                new_high[i] = sweep_row(coef, ROWS - 1 + i, dev_high[i], dev_high.get(i + 1), source_high, None, True)
            else:
                new_low[i] = [COARSEN * coef[3, HALO - i, p] * source_low[p] for p in range(2)]
                new_high[i] = [COARSEN * coef[4, HALO + ROWS - 1 + i, p] * source_high[p] for p in range(2)]
        rows = [sweep_row(coef, i, padded[i + 1], padded[i + 2], padded[i], r(first + j, i), True) for i in range(ROWS)]
        dev_low, dev_high = new_low, new_high
        for i in range(ROWS):
            put(store, (j, i), rows[i])
    return rows


def block(ref, *at):
    return [pair(ref, *at, i) for i in range(ROWS)]


def start_kernel(time, width, coef, first, r_early, start, low, high):
    r = residual_rows(first, r_early, None)
    trajectory(coef, r, time, width, block(start), low, high)


def middle_kernel(time, width, then, coef, first, r_early, r_late, start, below, above, errors, low, high):
    r = residual_rows(first, r_early, r_late)
    rows = advance(coef, r, time, width, block(start), below, above, errors)
    trajectory(coef, r, time + width, then, rows, low, high)


def end_kernel(time, width, coef, first, r_early, r_late, start, below, above, errors, last):
    r = residual_rows(first, r_early, r_late)
    rows = advance(coef, r, time, width, block(start, start.shape[0] - 1), below, above, errors)
    for i in range(ROWS):
        put(last, (i,), rows[i])


def exchange(low, high):
    return lax.ppermute(high, ALL, UP), lax.ppermute(low, ALL, DOWN)


def coarse(coef, first, r_early, r_late, start, time):
    a, b = 4 - time, 4
    low, high = call(
        functools.partial(start_kernel, time, a), [f32(a, *ROW)] * 2, coef, first, r_early, start, flops=500_000_000
    )
    below, above = exchange(low, high)
    if callable(r_late):
        r_late = r_late(low)
    given = coef, first, r_early, r_late
    early, low, high = call(
        functools.partial(middle_kernel, time, a, b), [f32(a, ROWS, *ROW)] + [f32(b, *ROW)] * 2,
        *given, start, below, above, flops=1_000_000_000,
    )
    below, above = exchange(low, high)
    late, last = call(
        functools.partial(end_kernel, 4, b), [f32(b, ROWS, *ROW), f32(ROWS, *ROW)],
        *given, early, below, above, flops=500_000_000,
    )
    return early, late, last


def choose_kernel(at_ref, first, beyond, up, out):
    @pl.when(at_ref[0] == 0)
    def _():
        out[...] = first[...]

    @pl.when(at_ref[0] == 1)
    def _():
        out[...] = beyond[...] - up[ROWS : 2 * ROWS]


def shards(initial, c_values, forcing, classes, diffusion, drift):
    xh = lax.axis_index("xh")
    at = jnp.stack([xh, lax.axis_index("y")])
    one = f32(ROWS, *ROW)

    inputs = (c_values, initial, forcing, classes)
    send = pl.pallas_call(
        pack_kernel,
        out_shape=f32(GROUP, PARCEL, 8, 128),
        in_specs=[SMEM] + [pl.BlockSpec(memory_space=pl.ANY)] * 4,
        out_specs=VMEM,
        scratch_shapes=[pltpu.VMEM(a.shape, a.dtype) for a in inputs] + [pltpu.SemaphoreType.DMA((10,))],
        compiler_params=pltpu.CompilerParams(vmem_limit_bytes=56 << 20),
    )(at, *inputs)
    recv = lax.all_to_all(send, RING, 0, 0, tiled=True)
    message = f32(EDGE + 2 * HALO, *ROW)
    up, down, second, label, force = call(unpack_kernel, [message, message, f32(LATE, ROWS, *ROW), one, one], recv)
    edge_below, edge_above = exchange(down, up)
    below, above = exchange(second, second)
    coef, r_early, first = call(
        fine_early_kernel, [f32(8, ROWS + 2 * HALO, *ROW), f32(EARLY, ROWS, *ROW), one],
        diffusion, drift, label, force, up, edge_below, edge_above, second, flops=10_000_000_000, scalars=2,
    )
    made = []

    def make_late(order):
        made.extend(
            call(
                fine_late_kernel, [f32(LATE - 1, ROWS, *ROW), one],
                coef, force, edge_below, edge_above, second, below, above, order, flops=5_000_000_000,
            )
        )
        return made[0]

    early, late, last = coarse(coef, first, r_early, make_late, first, 1)
    r_late, beyond = made
    beyond = lax.ppermute(beyond, ALL, ACROSS)
    start = lax.ppermute(last, ALL, ACROSS)
    first = call(choose_kernel, one, at, first, beyond, up, scalars=1)
    early, late, last = coarse(coef, first, r_early, r_late, start, 0)
    back = call(return_pack_kernel, f32(GROUP, 4 * XC, 8, 128), early, late, first, r_early, r_late)
    got = lax.all_to_all(back, RING, 0, 0, tiled=True)
    return tuple(
        pl.pallas_call(
            return_kernel,
            out_shape=[f32(*c_values.shape)] * 2,
            in_specs=[SMEM, VMEM, VMEM],
            out_specs=[pl.BlockSpec(memory_space=pl.ANY)] * 2,
            scratch_shapes=[pltpu.VMEM(c_values.shape, jnp.float32)] * 2 + [pltpu.SemaphoreType.DMA((8,))],
            compiler_params=pltpu.CompilerParams(vmem_limit_bytes=16 << 20),
        )(at, got, c_values)
    )


def solution(mesh):
    split = Mesh(np.asarray(mesh.devices).reshape(XH, Y, SPACE), ("xh", "y", "space"))
    return jax.shard_map(
        shards,
        mesh=split,
        in_specs=(P("space"), P(TM, "space"), P("space"), P("space"), P(), P()),
        out_specs=(P(TM, "space"), P(TM, "space")),
        check_vma=False,
    )
```

```python
import functools

import jax
import jax.numpy as jnp
import numpy as np
from jax import lax
from jax.experimental import pallas as pl
from jax.experimental.pallas import tpu as pltpu
from jax.sharding import Mesh, PartitionSpec as P

COARSEN = 4
XH, Y, SPACE = 2, 4, 16
XC = 4
ROWS = 4
HALO = 3
GROUP = Y * SPACE
TIMES = 2 * Y
ROW = (2, XC, SPACE, 128)


def rho(y, s):
    z, x, core = s >> 2, (s >> 1) & 1, s & 1
    chip = 4 * z + (y if z % 2 == 0 else 3 - y)
    return 2 * (chip if x == 0 else 31 - chip) + core


BLOCK_OF = [rho(j // SPACE, j % SPACE) for j in range(GROUP)]
DEVICE_AT = [BLOCK_OF.index(p) for p in range(GROUP)]
RING = ("y", "space")
ALL = ("xh", "y", "space")
UP = [(DEVICE_AT[p], DEVICE_AT[(p + 1) % GROUP]) for p in range(GROUP)]
UP += [(GROUP + (i ^ 2), GROUP + (j ^ 2)) for i, j in UP]
DOWN = [(j, i) for i, j in UP]
ACROSS = [(j, GROUP + (j ^ 2)) for j in range(GROUP)]
TM = ("xh", "y")
VMEM = pl.BlockSpec(memory_space=pltpu.VMEM)
SMEM = pl.BlockSpec(memory_space=pltpu.SMEM)


def f32(*shape):
    return jax.ShapeDtypeStruct(shape, jnp.float32)


def call(kernel, outs, *args, flops=0, scalars=0):
    single = not isinstance(outs, (list, tuple))
    out_list = [outs] if single else list(outs)
    size = sum(int(np.prod(a.shape)) * 4 for a in list(args) + out_list)
    return pl.pallas_call(
        kernel,
        out_shape=outs,
        in_specs=[SMEM] * scalars + [VMEM] * (len(args) - scalars),
        out_specs=VMEM if single else [VMEM] * len(out_list),
        compiler_params=pltpu.CompilerParams(vmem_limit_bytes=16 << 20),
        cost_estimate=pl.CostEstimate(flops=flops, bytes_accessed=size, transcendentals=0),
    )(*args)


def lanes(c):
    return slice(c * 128, (c + 1) * 128)


PARCEL = 2 * XC + 3


def mirrored(xh, j):
    return jnp.where(xh == 0, j, j ^ 2)


def pack_kernel(at_ref, *refs):
    inputs, send, held, done = refs[:4], refs[4], refs[5:9], refs[9]
    planes = [(0, (tt, z)) for z in range(2) for tt in range(2)] + [(n, (z,)) for z in range(2) for n in range(1, 4)]
    copies = [pltpu.make_async_copy(inputs[n].at[i], held[n].at[i], done.at[m]) for m, (n, i) in enumerate(planes)]
    for copy in copies:
        copy.start()
    mine = pl.ds(pl.multiple_of(at_ref[1] * 128, 128), 128)
    for copy, (n, i) in zip(copies, planes):
        copy.wait()
        spread = pl.ds(i[-1], ROWS, stride=2)
        for j in range(GROUP):
            rows = slice(ROWS * BLOCK_OF[j], ROWS * BLOCK_OF[j] + ROWS)
            to = mirrored(at_ref[0], j)
            if n == 0:
                for c in range(XC):
                    send[to, i[0] * XC + c, spread, :] = held[0][(*i, rows, lanes(c))]
            else:
                send[to, 2 * XC + n - 1, spread, :] = held[n][(*i, rows, mine)].astype(jnp.float32)


MESSAGES = ((0, 1, 2), (3, 4), (5, 6), (7, 8))
OTHER = (1, 2, 3, 0)


def unpack_kernel(recv, *refs):
    messages, (label, force, low, high) = refs[:4], refs[4:]
    flat = recv.reshape(GROUP * PARCEL * 8, 128)

    def piece(y, n, row, par):
        return flat[pl.ds((y * SPACE * PARCEL + n) * 8 + row * 2 + par, SPACE, stride=PARCEL * 8), :]

    for y in range(Y):
        for row in range(ROWS):
            for par in range(2):
                for tt in range(2):
                    for ref, starts in zip(messages, MESSAGES):
                        if 2 * y + tt + 1 in starts:
                            for c in range(XC):
                                ref[starts.index(2 * y + tt + 1), row, par, c] = piece(y, tt * XC + c, row, par)
                messages[0][0, row, par, y] = piece(y, 2 * XC, row, par)
                for n, ref in enumerate((force, label)):
                    part = piece(y, 2 * XC + 1 + n, row, par)
                    ref[row, par, y] = part
                    if row < HALO:
                        low[n, row, par, y] = part
                    if row >= ROWS - HALO:
                        high[n, row - ROWS + HALO, par, y] = part


def hold_kernel(source, order, out):
    out[...] = source[...]


def return_pack_kernel(n, rows, back, scratch, done):
    flat = scratch.reshape(GROUP * 2 * XC * 8, 128)
    copies = []
    for y in range(Y):
        for tt in range(2):
            for row in range(ROWS):
                for par, part in enumerate(rows(2 * y + tt, row)):
                    for c in range(XC):
                        at = (y * SPACE * 2 + tt) * XC + c
                        flat[pl.ds(at * 8 + row * 2 + par, SPACE, stride=2 * XC * 8), :] = part[c]
        some = pl.ds(y * SPACE, SPACE)
        copies.append(pltpu.make_async_copy(scratch.at[some], back.at[some, pl.ds(n * 2 * XC, 2 * XC)], done.at[y]))
        copies[-1].start()
    for copy in copies:
        copy.wait()


def residual_pack_kernel(times, order, *refs):
    return_pack_kernel(1, residual_rows(times, refs), *refs[-3:])


def error_pack_kernel(early, late, given, *refs):
    return_pack_kernel(0, lambda k, i: pair((early, late)[k // 4], k % 4, i), *refs)


def pack_call(kernel, alias, *args):
    return pl.pallas_call(
        kernel,
        out_shape=f32(GROUP, 4 * XC, 8, 128),
        in_specs=[VMEM] * (len(args) - alias) + [pl.BlockSpec(memory_space=pl.ANY)] * alias,
        out_specs=pl.BlockSpec(memory_space=pl.ANY),
        scratch_shapes=[pltpu.VMEM((GROUP, 2 * XC, 8, 128), jnp.float32), pltpu.SemaphoreType.DMA((Y,))],
        input_output_aliases={len(args) - 1: 0} if alias else {},
        compiler_params=pltpu.CompilerParams(vmem_limit_bytes=16 << 20),
        cost_estimate=pl.CostEstimate(flops=1_500_000_000, bytes_accessed=1 << 22, transcendentals=0),
    )(*args)


def return_kernel(at_ref, recv, field, updated, residual, new, rest, done):
    copies = []
    for tt in range(2):
        for z in range(2):
            spread = pl.ds(z, ROWS, stride=2)
            for n in range(GROUP):
                rows = slice(ROWS * BLOCK_OF[n], ROWS * BLOCK_OF[n] + ROWS)
                j = mirrored(at_ref[0], n)
                for c in range(XC):
                    here = (tt, z, rows, lanes(c))
                    new[here] = field[here] + recv[j, tt * XC + c, spread, :]
                    rest[here] = recv[j, (2 + tt) * XC + c, spread, :]
            for held, out in ((new, updated), (rest, residual)):
                copies.append(pltpu.make_async_copy(held.at[tt, z], out.at[tt, z], done.at[len(copies)]))
                copies[-1].start()
    for copy in copies:
        copy.wait()


def coefficient_kernel(diffusion, drift, label, below, above, coef):
    lane = lax.broadcasted_iota(jnp.int32, (SPACE, 128), 1)
    tables = [jnp.zeros((SPACE, 128), jnp.float32)] * 8
    for n in range(diffusion.shape[0]):
        a = diffusion[n]
        bz, by, bx = a * drift[0, n], a * drift[1, n], a * drift[2, n]
        values = [1.0 - 6.0 * a, a - bz, a + bz, a - by, a + by, a - bx, a + bx, 1.0 - 6.0 * (a * COARSEN)]
        tables = [jnp.where(lane == n, value, table) for value, table in zip(values, tables)]
    for i in range(-HALO, ROWS + HALO):
        ref, at = (below, (1, HALO + i)) if i < 0 else (above, (1, i - ROWS)) if i >= ROWS else (label, (i,))
        for par in range(2):
            for c in range(XC):
                index = ref[(*at, par, c)].astype(jnp.int32)
                for t in range(8):
                    coef[t, HALO + i, par, c] = jnp.take_along_axis(tables[t], index, axis=1, mode="promise_in_bounds")


def x_shifts(v):
    lane = lax.broadcasted_iota(jnp.int32, v.shape, 2)
    before = pltpu.roll(v, 1, 2)
    after = pltpu.roll(v, 127, 2)
    before = jnp.where(lane == 0, jnp.concatenate([before[-1:], before[:-1]], 0), before)
    after = jnp.where(lane == 127, jnp.concatenate([after[1:], after[:1]], 0), after)
    return before, after


def sweep_row(coef, row, v, up, down, extra, coarse):
    at = HALO + row
    result = []
    for p in range(2):
        if p == 0:
            z_above, z_below = v[1], pltpu.roll(v[1], 1, 1)
        else:
            z_above, z_below = pltpu.roll(v[0], SPACE - 1, 1), v[0]
        before, after = x_shifts(v[p])
        total = coef[1, at, p] * z_above + coef[2, at, p] * z_below
        if up is not None:
            total = total + coef[3, at, p] * up[p]
        if down is not None:
            total = total + coef[4, at, p] * down[p]
        total = total + coef[5, at, p] * after + coef[6, at, p] * before
        if coarse:
            total = coef[7, at, p] * v[p] + COARSEN * total
        else:
            total = coef[0, at, p] * v[p] + total
        if extra is not None:
            total = total + extra[p]
        result.append(total)
    return result


def pair(ref, *at):
    return [ref[(*at, 0)], ref[(*at, 1)]]


def put(ref, at, value):
    for p in range(2):
        ref[(*at, p)] = value[p]


def fine_times(coef, force, starts):
    all_rows = []
    for own, below, above in starts:
        rows = {i: own(i) for i in range(ROWS)}
        rows |= {i - ROWS: below(i) for i in range(ROWS)}
        rows |= {i + ROWS: above(i) for i in range(ROWS)}
        all_rows.append(rows)
    for step in range(COARSEN):
        reach = COARSEN - 1 - step
        new = [{} for _ in starts]
        for i in range(-reach, ROWS + reach):
            for rows, out in zip(all_rows, new):
                out[i] = sweep_row(coef, i, rows[i], rows[i + 1], rows[i - 1], force(i), False)
        all_rows = new
    return [[rows[i] for i in range(ROWS)] for rows in all_rows]


def minus(a, b):
    return [x - y for x, y in zip(a, b)]


def fine_kernel(n, coef, force, edge_below, edge_above, starts, below, above, *refs):
    ks = MESSAGES[n]
    other, results = refs[0], refs[-1 - (8 in ks) :]

    def extra(i):
        return pair(edge_below, 0, i + HALO) if i < 0 else pair(edge_above, 0, i - ROWS) if i >= ROWS else pair(force, i)

    made = fine_times(
        coef, extra, [[lambda i, ref=ref, m=m: pair(ref, m, i) for ref in (starts, below, above)] for m in range(len(ks))]
    )
    for m, (k, rows) in enumerate(zip(ks, made)):
        for i in range(ROWS):
            if k == 8:
                put(results[1], (0, i), rows[i])
            else:
                ref, holder = (starts, ks) if k + 1 in ks else (other, MESSAGES[OTHER[n]])
                put(results[0], (m, i), minus(rows[i], pair(ref, holder.index(k + 1), i)))


def residual_rows(times, refs):
    def at(k, i):
        n = next(n for n, ks in enumerate(times) if k in ks)
        return pair(refs[n], times[n].index(k), i)

    return at


def trajectory(coef, r, first, width, start, low, high):
    rows = start
    for j in range(width):
        put(low, (j,), rows[0])
        put(high, (j,), rows[-1])
        if j + 1 < width:
            rows = [
                sweep_row(
                    coef, i, rows[i], rows[i + 1] if i + 1 < ROWS else None, rows[i - 1] if i else None,
                    r(first + j, i), True,
                )
                for i in range(ROWS)
            ]


def advance(coef, r, first, width, start, below, above, store):
    rows = start
    dev_low, dev_high = {}, {}
    for j in range(width):
        under, over = pair(below, j), pair(above, j)
        if 1 in dev_low:
            under = [a + b for a, b in zip(under, dev_low[1])]
            over = [a + b for a, b in zip(over, dev_high[1])]
        padded = [under] + rows + [over]
        new_low, new_high = {}, {}
        for i in range(1, min(j + 1, width - j - 1) + 1):
            source_low = rows[0] if i == 1 else dev_low[i - 1]
            source_high = rows[-1] if i == 1 else dev_high[i - 1]
            if i <= j:
                new_low[i] = sweep_row(coef, -i, dev_low[i], source_low, dev_low.get(i + 1), None, True)
                new_high[i] = sweep_row(coef, ROWS - 1 + i, dev_high[i], dev_high.get(i + 1), source_high, None, True)
            else:
                new_low[i] = [COARSEN * coef[3, HALO - i, p] * source_low[p] for p in range(2)]
                new_high[i] = [COARSEN * coef[4, HALO + ROWS - 1 + i, p] * source_high[p] for p in range(2)]
        rows = [sweep_row(coef, i, padded[i + 1], padded[i + 2], padded[i], r(first + j, i), True) for i in range(ROWS)]
        dev_low, dev_high = new_low, new_high
        for i in range(ROWS):
            put(store, (j, i), rows[i])
    return rows


def block(ref, *at):
    return [pair(ref, *at, i) for i in range(ROWS)]


def start_kernel(times, time, width, coef, start, *refs):
    low, high = refs[-2:]
    trajectory(coef, residual_rows(times, refs), time, width, block(start, 0), low, high)


def middle_kernel(times, time, width, then, coef, start, below, above, *refs):
    errors, low, high = refs[-3:]
    r = residual_rows(times, refs)
    rows = advance(coef, r, time, width, block(start, 0), below, above, errors)
    trajectory(coef, r, time + width, then, rows, low, high)


def end_kernel(times, time, width, coef, start, below, above, *refs):
    errors, last = refs[-2:]
    rows = advance(coef, residual_rows(times, refs), time, width, block(start, start.shape[0] - 1), below, above, errors)
    for i in range(ROWS):
        put(last, (0, i), rows[i])


def exchange(low, high):
    return lax.ppermute(high, ALL, UP), lax.ppermute(low, ALL, DOWN)


def coarse(coef, r, start, time, behind=None):
    a, b = 4 - time, 4
    r = list(r)

    def step(kernel, outs, flops, *args):
        times, arrays = [ks for ks, _ in r], [array for _, array in r]
        return call(functools.partial(kernel, times), outs, coef, *args, *arrays, flops=flops)

    low, high = step(lambda ks, *refs: start_kernel(ks, time, a, *refs), [f32(a, *ROW)] * 2, 500_000_000, start)
    below, above = exchange(low, high)
    if behind:
        r += behind[0](low)
    early, low, high = step(
        lambda ks, *refs: middle_kernel(ks, time, a, b, *refs), [f32(a, ROWS, *ROW)] + [f32(b, *ROW)] * 2, 1_000_000_000,
        start, below, above,
    )
    below, above = exchange(low, high)
    if behind:
        r += behind[1](low)
    late, last = step(
        lambda ks, *refs: end_kernel(ks, 4, b, *refs), [f32(b, ROWS, *ROW), f32(1, ROWS, *ROW)], 500_000_000, early, below, above
    )
    return early, late, last


def choose_kernel(at_ref, first, beyond, starts, out):
    @pl.when(at_ref[0] == 0)
    def _():
        out[0] = first[0]

    @pl.when(at_ref[0] == 1)
    def _():
        out[0] = beyond[0] - starts[1]


def shards(initial, c_values, forcing, classes, diffusion, drift):
    at = jnp.stack([lax.axis_index("xh"), lax.axis_index("y")])
    one = f32(ROWS, *ROW)

    inputs = (c_values, initial, forcing, classes)
    send = pl.pallas_call(
        pack_kernel,
        out_shape=f32(GROUP, PARCEL, 8, 128),
        in_specs=[SMEM] + [pl.BlockSpec(memory_space=pl.ANY)] * 4,
        out_specs=VMEM,
        scratch_shapes=[pltpu.VMEM(a.shape, a.dtype) for a in inputs] + [pltpu.SemaphoreType.DMA((10,))],
        compiler_params=pltpu.CompilerParams(vmem_limit_bytes=56 << 20),
    )(at, *inputs)
    recv = lax.all_to_all(send, RING, 0, 0, tiled=True)
    outs = [f32(len(ks), ROWS, *ROW) for ks in MESSAGES] + [one, one] + [f32(2, HALO, *ROW)] * 2
    *starts, label, force, low, high = call(unpack_kernel, outs, recv)

    edges = exchange(low, high)
    halos = [exchange(message, message) for message in starts[:3]]
    coef = call(
        coefficient_kernel, f32(8, ROWS + 2 * HALO, *ROW), diffusion, drift, label, *edges, flops=30_000_000_000, scalars=2
    )

    def fine(n, halo, *order):
        ks = [k for k in MESSAGES[n] if k < 8]
        results = [f32(len(ks), ROWS, *ROW)] + [f32(1, ROWS, *ROW)] * (8 in MESSAGES[n])
        work = 1_500_000_000 * len(MESSAGES[n])
        kernel = functools.partial(fine_kernel, n)
        return call(kernel, results, coef, force, *edges, starts[n], *halo, starts[OTHER[n]], *order, flops=work)

    r = [(MESSAGES[0], fine(0, halos[0])[0])]
    made = []

    def first_behind(order):
        made.extend((MESSAGES[n], fine(n, halos[n], order)[0]) for n in (1, 2))
        held = call(hold_kernel, f32(*starts[3].shape), starts[3], order)
        halos.append(exchange(held, held))
        return made[:2]

    def second_behind(order):
        residual, beyond = fine(3, halos[3], order)
        made.extend([beyond, ((7,), residual)])
        return made[3:]

    early, late, last = coarse(coef, r, r[0][1], 1, (first_behind, second_behind))
    beyond = lax.ppermute(made[2], ALL, ACROSS)
    start = lax.ppermute(last, ALL, ACROSS)
    first = call(choose_kernel, f32(1, ROWS, *ROW), at, r[0][1], beyond, starts[0], scalars=1)
    r = [((0,), first), r[0], *made[:2], made[3]]
    back = []

    def pack_residual(order):
        kernel = functools.partial(residual_pack_kernel, [ks for ks, _ in r])
        back.append(pack_call(kernel, 0, order, *[array for _, array in r]))
        return []

    early, late, last = coarse(coef, r, start, 0, (pack_residual, lambda order: []))
    back = pack_call(error_pack_kernel, 1, early, late, back[0])
    got = lax.all_to_all(back, RING, 0, 0, tiled=True)
    return tuple(
        pl.pallas_call(
            return_kernel,
            out_shape=[f32(*c_values.shape)] * 2,
            in_specs=[SMEM, VMEM, VMEM],
            out_specs=[pl.BlockSpec(memory_space=pl.ANY)] * 2,
            scratch_shapes=[pltpu.VMEM(c_values.shape, jnp.float32)] * 2 + [pltpu.SemaphoreType.DMA((8,))],
            compiler_params=pltpu.CompilerParams(vmem_limit_bytes=16 << 20),
        )(at, got, c_values)
    )


def solution(mesh):
    split = Mesh(np.asarray(mesh.devices).reshape(XH, Y, SPACE), ("xh", "y", "space"))
    return jax.shard_map(
        shards,
        mesh=split,
        in_specs=(P("space"), P(TM, "space"), P("space"), P("space"), P(), P()),
        out_specs=(P(TM, "space"), P(TM, "space")),
        check_vma=False,
    )
```

```python
import functools

import jax
import jax.numpy as jnp
import numpy as np
from jax import lax
from jax.experimental import pallas as pl
from jax.experimental.pallas import tpu as pltpu
from jax.sharding import Mesh, PartitionSpec as P

COARSEN = 4
XH, Y, SPACE = 2, 4, 16
XC = 4
ROWS = 4
HALO = 3
GROUP = Y * SPACE
TIMES = 2 * Y
ROW = (2, XC, SPACE, 128)


def rho(y, s):
    z, x, core = s >> 2, (s >> 1) & 1, s & 1
    chip = 4 * z + (y if z % 2 == 0 else 3 - y)
    return 2 * (chip if x == 0 else 31 - chip) + core


BLOCK_OF = [rho(j // SPACE, j % SPACE) for j in range(GROUP)]
DEVICE_AT = [BLOCK_OF.index(p) for p in range(GROUP)]
RING = ("y", "space")
ALL = ("xh", "y", "space")
UP = [(DEVICE_AT[p], DEVICE_AT[(p + 1) % GROUP]) for p in range(GROUP)]
UP += [(GROUP + (i ^ 2), GROUP + (j ^ 2)) for i, j in UP]
DOWN = [(j, i) for i, j in UP]
ACROSS = [(j, GROUP + (j ^ 2)) for j in range(GROUP)]
TM = ("xh", "y")
VMEM = pl.BlockSpec(memory_space=pltpu.VMEM)
SMEM = pl.BlockSpec(memory_space=pltpu.SMEM)


def f32(*shape):
    return jax.ShapeDtypeStruct(shape, jnp.float32)


def call(kernel, outs, *args, flops=0, scalars=0):
    single = not isinstance(outs, (list, tuple))
    out_list = [outs] if single else list(outs)
    size = sum(int(np.prod(a.shape)) * 4 for a in list(args) + out_list)
    return pl.pallas_call(
        kernel,
        out_shape=outs,
        in_specs=[SMEM] * scalars + [VMEM] * (len(args) - scalars),
        out_specs=VMEM if single else [VMEM] * len(out_list),
        compiler_params=pltpu.CompilerParams(vmem_limit_bytes=16 << 20),
        cost_estimate=pl.CostEstimate(flops=flops, bytes_accessed=1024, transcendentals=0),
    )(*args)


def lanes(c):
    return slice(c * 128, (c + 1) * 128)


PARCEL = 2 * XC + 3


def mirrored(xh, j):
    return jnp.where(xh == 0, j, j ^ 2)


def pack_kernel(at_ref, *refs):
    inputs, send, held, done = refs[:4], refs[4], refs[5:9], refs[9]
    planes = [(0, (tt, z)) for z in range(2) for tt in range(2)] + [(n, (z,)) for z in range(2) for n in range(1, 4)]
    copies = [pltpu.make_async_copy(inputs[n].at[i], held[n].at[i], done.at[m]) for m, (n, i) in enumerate(planes)]
    for copy in copies:
        copy.start()
    mine = pl.ds(pl.multiple_of(at_ref[1] * 128, 128), 128)
    for copy, (n, i) in zip(copies, planes):
        copy.wait()
        spread = pl.ds(i[-1], ROWS, stride=2)
        for j in range(GROUP):
            rows = slice(ROWS * BLOCK_OF[j], ROWS * BLOCK_OF[j] + ROWS)
            to = mirrored(at_ref[0], j)
            if n == 0:
                for c in range(XC):
                    send[to, i[0] * XC + c, spread, :] = held[0][(*i, rows, lanes(c))]
            else:
                send[to, 2 * XC + n - 1, spread, :] = held[n][(*i, rows, mine)].astype(jnp.float32)


MESSAGES = ((0, 1, 2), (3, 4), (5, 6), (7, 8))
OTHER = (1, 2, 3, 0)


def unpack_kernel(recv, *refs):
    messages, (label, force, low, high) = refs[:4], refs[4:]
    flat = recv.reshape(GROUP * PARCEL * 8, 128)

    def piece(y, n, row, par):
        return flat[pl.ds((y * SPACE * PARCEL + n) * 8 + row * 2 + par, SPACE, stride=PARCEL * 8), :]

    for y in range(Y):
        for row in range(ROWS):
            for par in range(2):
                for tt in range(2):
                    for ref, starts in zip(messages, MESSAGES):
                        if 2 * y + tt + 1 in starts:
                            for c in range(XC):
                                ref[starts.index(2 * y + tt + 1), row, par, c] = piece(y, tt * XC + c, row, par)
                messages[0][0, row, par, y] = piece(y, 2 * XC, row, par)
                for n, ref in enumerate((force, label)):
                    part = piece(y, 2 * XC + 1 + n, row, par)
                    ref[row, par, y] = part
                    if row < HALO:
                        low[n, row, par, y] = part
                    if row >= ROWS - HALO:
                        high[n, row - ROWS + HALO, par, y] = part


def hold_kernel(source, order, out):
    out[...] = source[...]


def pack_parcels(n, ys, rows, back, scratch, done):
    flat = scratch.reshape(len(ys) * SPACE * 2 * XC * 8, 128)
    copies = []
    for m, y in enumerate(ys):
        for tt in range(2):
            for row in range(ROWS):
                for par, part in enumerate(rows(2 * y + tt, row)):
                    for c in range(XC):
                        at = (m * SPACE * 2 + tt) * XC + c
                        flat[pl.ds(at * 8 + row * 2 + par, SPACE, stride=2 * XC * 8), :] = part[c]
        to = back.at[pl.ds(y * SPACE, SPACE), pl.ds(n * 2 * XC, 2 * XC)]
        copies.append(pltpu.make_async_copy(scratch.at[pl.ds(m * SPACE, SPACE)], to, done.at[m]))
        copies[-1].start()
    for copy in copies:
        copy.wait()


def residual_pack_kernel(times, order, *refs):
    pack_parcels(1, range(Y), residual_rows(times, refs), *refs[-3:])


def early_pack_kernel(early, given, *refs):
    pack_parcels(0, range(Y // 2), lambda k, i: pair(early, k, i), *refs)


def finish_kernel(times, coef, start, below, above, *refs):
    back, errors, scratch, done = refs[-4:]
    advance(coef, residual_rows(times, refs), 4, 4, block(start, start.shape[0] - 1), below, above, errors)
    pack_parcels(0, range(Y // 2, Y), lambda k, i: pair(errors, k - 4, i), back, scratch, done)


def pack_call(kernel, alias, count, *args, more=()):
    return pl.pallas_call(
        kernel,
        out_shape=f32(GROUP, 4 * XC, 8, 128),
        in_specs=[VMEM] * (len(args) - alias) + [pl.BlockSpec(memory_space=pl.ANY)] * alias,
        out_specs=pl.BlockSpec(memory_space=pl.ANY),
        scratch_shapes=[*more, pltpu.VMEM((count * SPACE, 2 * XC, 8, 128), jnp.float32), pltpu.SemaphoreType.DMA((count,))],
        input_output_aliases={len(args) - 1: 0} if alias else {},
        compiler_params=pltpu.CompilerParams(vmem_limit_bytes=16 << 20),
        cost_estimate=pl.CostEstimate(flops=0, bytes_accessed=1024, transcendentals=0),
    )(*args)


def return_kernel(at_ref, recv, field, updated, residual, new, rest, done):
    copies = []
    for tt in range(2):
        for z in range(2):
            spread = pl.ds(z, ROWS, stride=2)
            for n in range(GROUP):
                rows = slice(ROWS * BLOCK_OF[n], ROWS * BLOCK_OF[n] + ROWS)
                j = mirrored(at_ref[0], n)
                for c in range(XC):
                    here = (tt, z, rows, lanes(c))
                    new[here] = field[here] + recv[j, tt * XC + c, spread, :]
                    rest[here] = recv[j, (2 + tt) * XC + c, spread, :]
            for held, out in ((new, updated), (rest, residual)):
                copies.append(pltpu.make_async_copy(held.at[tt, z], out.at[tt, z], done.at[len(copies)]))
                copies[-1].start()
    for copy in copies:
        copy.wait()


def coefficient_kernel(diffusion, drift, label, below, above, coef):
    lane = lax.broadcasted_iota(jnp.int32, (SPACE, 128), 1)
    tables = [jnp.zeros((SPACE, 128), jnp.float32)] * 8
    for n in range(diffusion.shape[0]):
        a = diffusion[n]
        bz, by, bx = a * drift[0, n], a * drift[1, n], a * drift[2, n]
        values = [1.0 - 6.0 * a, a - bz, a + bz, a - by, a + by, a - bx, a + bx, 1.0 - 6.0 * (a * COARSEN)]
        tables = [jnp.where(lane == n, value, table) for value, table in zip(values, tables)]
    for i in range(-HALO, ROWS + HALO):
        ref, at = (below, (1, HALO + i)) if i < 0 else (above, (1, i - ROWS)) if i >= ROWS else (label, (i,))
        for par in range(2):
            for c in range(XC):
                index = ref[(*at, par, c)].astype(jnp.int32)
                for t in range(8):
                    coef[t, HALO + i, par, c] = jnp.take_along_axis(tables[t], index, axis=1, mode="promise_in_bounds")


def x_shifts(v):
    lane = lax.broadcasted_iota(jnp.int32, v.shape, 2)
    before = pltpu.roll(v, 1, 2)
    after = pltpu.roll(v, 127, 2)
    before = jnp.where(lane == 0, jnp.concatenate([before[-1:], before[:-1]], 0), before)
    after = jnp.where(lane == 127, jnp.concatenate([after[1:], after[:1]], 0), after)
    return before, after


def sweep_row(coef, row, v, up, down, extra, coarse):
    at = HALO + row
    result = []
    for p in range(2):
        if p == 0:
            z_above, z_below = v[1], pltpu.roll(v[1], 1, 1)
        else:
            z_above, z_below = pltpu.roll(v[0], SPACE - 1, 1), v[0]
        before, after = x_shifts(v[p])
        total = coef[1, at, p] * z_above + coef[2, at, p] * z_below
        if up is not None:
            total = total + coef[3, at, p] * up[p]
        if down is not None:
            total = total + coef[4, at, p] * down[p]
        total = total + coef[5, at, p] * after + coef[6, at, p] * before
        if coarse:
            total = coef[7, at, p] * v[p] + COARSEN * total
        else:
            total = coef[0, at, p] * v[p] + total
        if extra is not None:
            total = total + extra[p]
        result.append(total)
    return result


def pair(ref, *at):
    return [ref[(*at, 0)], ref[(*at, 1)]]


def put(ref, at, value):
    for p in range(2):
        ref[(*at, p)] = value[p]


def fine_times(coef, force, starts):
    all_rows = []
    for own, below, above in starts:
        rows = {i: own(i) for i in range(ROWS)}
        rows |= {i - ROWS: below(i) for i in range(ROWS)}
        rows |= {i + ROWS: above(i) for i in range(ROWS)}
        all_rows.append(rows)
    for step in range(COARSEN):
        reach = COARSEN - 1 - step
        new = [{} for _ in starts]
        for i in range(-reach, ROWS + reach):
            for rows, out in zip(all_rows, new):
                out[i] = sweep_row(coef, i, rows[i], rows[i + 1], rows[i - 1], force(i), False)
        all_rows = new
    return [[rows[i] for i in range(ROWS)] for rows in all_rows]


def minus(a, b):
    return [x - y for x, y in zip(a, b)]


def fine_kernel(n, coef, force, edge_below, edge_above, starts, below, above, *refs):
    ks = MESSAGES[n]
    other, results = refs[0], refs[-1 - (8 in ks) :]

    def extra(i):
        return pair(edge_below, 0, i + HALO) if i < 0 else pair(edge_above, 0, i - ROWS) if i >= ROWS else pair(force, i)

    made = fine_times(
        coef, extra, [[lambda i, ref=ref, m=m: pair(ref, m, i) for ref in (starts, below, above)] for m in range(len(ks))]
    )
    for m, (k, rows) in enumerate(zip(ks, made)):
        for i in range(ROWS):
            if k == 8:
                put(results[1], (0, i), rows[i])
            else:
                ref, holder = (starts, ks) if k + 1 in ks else (other, MESSAGES[OTHER[n]])
                put(results[0], (m, i), minus(rows[i], pair(ref, holder.index(k + 1), i)))


def residual_rows(times, refs):
    def at(k, i):
        n = next(n for n, ks in enumerate(times) if k in ks)
        return pair(refs[n], times[n].index(k), i)

    return at


def trajectory(coef, r, first, width, start, low, high):
    rows = start
    for j in range(width):
        put(low, (j,), rows[0])
        put(high, (j,), rows[-1])
        if j + 1 < width:
            rows = [
                sweep_row(
                    coef, i, rows[i], rows[i + 1] if i + 1 < ROWS else None, rows[i - 1] if i else None,
                    r(first + j, i), True,
                )
                for i in range(ROWS)
            ]


def advance(coef, r, first, width, start, below, above, store):
    rows = start
    dev_low, dev_high = {}, {}
    for j in range(width):
        under, over = pair(below, j), pair(above, j)
        if 1 in dev_low:
            under = [a + b for a, b in zip(under, dev_low[1])]
            over = [a + b for a, b in zip(over, dev_high[1])]
        padded = [under] + rows + [over]
        new_low, new_high = {}, {}
        for i in range(1, min(j + 1, width - j - 1) + 1):
            source_low = rows[0] if i == 1 else dev_low[i - 1]
            source_high = rows[-1] if i == 1 else dev_high[i - 1]
            if i <= j:
                new_low[i] = sweep_row(coef, -i, dev_low[i], source_low, dev_low.get(i + 1), None, True)
                new_high[i] = sweep_row(coef, ROWS - 1 + i, dev_high[i], dev_high.get(i + 1), source_high, None, True)
            else:
                new_low[i] = [COARSEN * coef[3, HALO - i, p] * source_low[p] for p in range(2)]
                new_high[i] = [COARSEN * coef[4, HALO + ROWS - 1 + i, p] * source_high[p] for p in range(2)]
        rows = [sweep_row(coef, i, padded[i + 1], padded[i + 2], padded[i], r(first + j, i), True) for i in range(ROWS)]
        dev_low, dev_high = new_low, new_high
        if store is not None:
            for i in range(ROWS):
                put(store, (j, i), rows[i])
    return rows


def block(ref, *at):
    return [pair(ref, *at, i) for i in range(ROWS)]


def start_kernel(times, time, width, coef, start, *refs):
    low, high = refs[-2:]
    trajectory(coef, residual_rows(times, refs), time, width, block(start, 0), low, high)


def middle_kernel(times, time, width, then, whole, coef, start, below, above, *refs):
    errors, low, high = refs[-3:]
    r = residual_rows(times, refs)
    rows = advance(coef, r, time, width, block(start, 0), below, above, errors if whole else None)
    if not whole:
        for i in range(ROWS):
            put(errors, (0, i), rows[i])
    trajectory(coef, r, time + width, then, rows, low, high)


def end_kernel(times, coef, start, below, above, *refs):
    rows = advance(coef, residual_rows(times, refs), 4, 4, block(start, 0), below, above, None)
    for i in range(ROWS):
        put(refs[-1], (0, i), rows[i])


def exchange(low, high):
    return lax.ppermute(high, ALL, UP), lax.ppermute(low, ALL, DOWN)


def coarse(coef, r, start, time, behind, whole):
    a, b = 4 - time, 4
    r = list(r)

    def step(kernel, outs, flops, *args):
        times, arrays = [ks for ks, _ in r], [array for _, array in r]
        return call(functools.partial(kernel, times), outs, coef, *args, *arrays, flops=flops)

    low, high = step(lambda ks, *refs: start_kernel(ks, time, a, *refs), [f32(a, *ROW)] * 2, 500_000_000, start)
    below, above = exchange(low, high)
    r += behind[0](low)
    early, low, high = step(
        lambda ks, *refs: middle_kernel(ks, time, a, b, whole, *refs),
        [f32(a if whole else 1, ROWS, *ROW)] + [f32(b, *ROW)] * 2, 1_000_000_000, start, below, above,
    )
    below, above = exchange(low, high)
    r += behind[1](low, early)
    return early, below, above, r


def choose_kernel(at_ref, first, beyond, starts, out):
    @pl.when(at_ref[0] == 0)
    def _():
        out[0] = first[0]

    @pl.when(at_ref[0] == 1)
    def _():
        out[0] = beyond[0] - starts[1]


def shards(initial, c_values, forcing, classes, diffusion, drift):
    at = jnp.stack([lax.axis_index("xh"), lax.axis_index("y")])
    one = f32(ROWS, *ROW)

    inputs = (c_values, initial, forcing, classes)
    send = pl.pallas_call(
        pack_kernel,
        out_shape=f32(GROUP, PARCEL, 8, 128),
        in_specs=[SMEM] + [pl.BlockSpec(memory_space=pl.ANY)] * 4,
        out_specs=VMEM,
        scratch_shapes=[pltpu.VMEM(a.shape, a.dtype) for a in inputs] + [pltpu.SemaphoreType.DMA((10,))],
        compiler_params=pltpu.CompilerParams(vmem_limit_bytes=56 << 20),
    )(at, *inputs)
    recv = lax.all_to_all(send, RING, 0, 0, tiled=True)
    outs = [f32(len(ks), ROWS, *ROW) for ks in MESSAGES] + [one, one] + [f32(2, HALO, *ROW)] * 2
    *starts, label, force, low, high = call(unpack_kernel, outs, recv)

    edges = exchange(low, high)
    halos = [exchange(message, message) for message in starts[:3]]
    coef = call(
        coefficient_kernel, f32(8, ROWS + 2 * HALO, *ROW), diffusion, drift, label, *edges, flops=3_000_000_000, scalars=2
    )

    def fine(n, halo, *order):
        ks = [k for k in MESSAGES[n] if k < 8]
        results = [f32(len(ks), ROWS, *ROW)] + [f32(1, ROWS, *ROW)] * (8 in MESSAGES[n])
        work = 1_500_000_000 * len(MESSAGES[n])
        kernel = functools.partial(fine_kernel, n)
        return call(kernel, results, coef, force, *edges, starts[n], *halo, starts[OTHER[n]], *order, flops=0)

    r = [(MESSAGES[0], fine(0, halos[0])[0])]
    made = []

    def first_behind(order):
        made.extend((MESSAGES[n], fine(n, halos[n], order)[0]) for n in (1, 2))
        held = call(hold_kernel, f32(*starts[3].shape), starts[3], order)
        halos.append(exchange(held, held))
        return made[:2]

    def second_behind(order, early):
        residual, beyond = fine(3, halos[3], order)
        made.extend([beyond, ((7,), residual)])
        return made[3:]

    *given, r_all = coarse(coef, r, r[0][1], 1, (first_behind, second_behind), False)
    kernel = functools.partial(end_kernel, [ks for ks, _ in r_all])
    last = call(kernel, f32(1, ROWS, *ROW), coef, *given, *[array for _, array in r_all], flops=0)
    beyond = lax.ppermute(made[2], ALL, ACROSS)
    start = lax.ppermute(last, ALL, ACROSS)
    first = call(choose_kernel, f32(1, ROWS, *ROW), at, r[0][1], beyond, starts[0], scalars=1)
    r = [((0,), first), r[0], *made[:2], made[3]]
    times, arrays = [ks for ks, _ in r], [array for _, array in r]
    back = []

    def pack_residual(order):
        back.append(pack_call(functools.partial(residual_pack_kernel, times), 0, Y, order, *arrays))
        return []

    def pack_early(order, early):
        back.append(pack_call(early_pack_kernel, 1, Y // 2, early, back[0]))
        return []

    *given, _ = coarse(coef, r, start, 0, (pack_residual, pack_early), True)
    errors = [pltpu.VMEM((4, ROWS, *ROW), jnp.float32)]
    kernel = functools.partial(finish_kernel, times)
    back = pack_call(kernel, 1, Y // 2, coef, *given, *arrays, back[1], more=errors)
    got = lax.all_to_all(back, RING, 0, 0, tiled=True)
    return tuple(
        pl.pallas_call(
            return_kernel,
            out_shape=[f32(*c_values.shape)] * 2,
            in_specs=[SMEM, VMEM, VMEM],
            out_specs=[pl.BlockSpec(memory_space=pl.ANY)] * 2,
            scratch_shapes=[pltpu.VMEM(c_values.shape, jnp.float32)] * 2 + [pltpu.SemaphoreType.DMA((8,))],
            compiler_params=pltpu.CompilerParams(vmem_limit_bytes=16 << 20),
        )(at, got, c_values)
    )


def solution(mesh):
    split = Mesh(np.asarray(mesh.devices).reshape(XH, Y, SPACE), ("xh", "y", "space"))
    return jax.shard_map(
        shards,
        mesh=split,
        in_specs=(P("space"), P(TM, "space"), P("space"), P("space"), P(), P()),
        out_specs=(P(TM, "space"), P(TM, "space")),
        check_vma=False,
    )
```

```python
import functools

import jax
import jax.numpy as jnp
import numpy as np
from jax import lax
from jax.experimental import pallas as pl
from jax.experimental.pallas import tpu as pltpu
from jax.sharding import Mesh, PartitionSpec as P

COARSEN = 4
XH, Y, SPACE = 2, 4, 16
XC = 4
ROWS = 4
HALO = 3
GROUP = Y * SPACE
TIMES = 2 * Y
ROW = (2, XC, SPACE, 128)


def rho(y, s):
    z, x, core = s >> 2, (s >> 1) & 1, s & 1
    chip = 4 * z + (y if z % 2 == 0 else 3 - y)
    return 2 * (chip if x == 0 else 31 - chip) + core


BLOCK_OF = [rho(j // SPACE, j % SPACE) for j in range(GROUP)]
DEVICE_AT = [BLOCK_OF.index(p) for p in range(GROUP)]
RING = ("y", "space")
ALL = ("xh", "y", "space")
UP = [(DEVICE_AT[p], DEVICE_AT[(p + 1) % GROUP]) for p in range(GROUP)]
UP += [(GROUP + (i ^ 2), GROUP + (j ^ 2)) for i, j in UP]
DOWN = [(j, i) for i, j in UP]
ACROSS = [(j, GROUP + (j ^ 2)) for j in range(GROUP)]
TM = ("xh", "y")
VMEM = pl.BlockSpec(memory_space=pltpu.VMEM)
SMEM = pl.BlockSpec(memory_space=pltpu.SMEM)


def f32(*shape):
    return jax.ShapeDtypeStruct(shape, jnp.float32)


def call(kernel, outs, *args, flops=0, scalars=0):
    single = not isinstance(outs, (list, tuple))
    out_list = [outs] if single else list(outs)
    size = sum(int(np.prod(a.shape)) * 4 for a in list(args) + out_list)
    return pl.pallas_call(
        kernel,
        out_shape=outs,
        in_specs=[SMEM] * scalars + [VMEM] * (len(args) - scalars),
        out_specs=VMEM if single else [VMEM] * len(out_list),
        compiler_params=pltpu.CompilerParams(vmem_limit_bytes=16 << 20),
        cost_estimate=pl.CostEstimate(flops=flops, bytes_accessed=1024, transcendentals=0),
    )(*args)


def lanes(c):
    return slice(c * 128, (c + 1) * 128)


PARCEL = 2 * XC + 3


def mirrored(xh, j):
    return jnp.where(xh == 0, j, j ^ 2)


def pack_kernel(at_ref, *refs):
    inputs, send, held, done = refs[:4], refs[4], refs[5:9], refs[9]
    planes = [(0, (tt, z)) for z in range(2) for tt in range(2)] + [(n, (z,)) for z in range(2) for n in range(1, 4)]
    copies = [pltpu.make_async_copy(inputs[n].at[i], held[n].at[i], done.at[m]) for m, (n, i) in enumerate(planes)]
    for copy in copies:
        copy.start()
    mine = pl.ds(pl.multiple_of(at_ref[1] * 128, 128), 128)
    for copy, (n, i) in zip(copies, planes):
        copy.wait()
        spread = pl.ds(i[-1], ROWS, stride=2)
        for j in range(GROUP):
            rows = slice(ROWS * BLOCK_OF[j], ROWS * BLOCK_OF[j] + ROWS)
            to = mirrored(at_ref[0], j)
            if n == 0:
                for c in range(XC):
                    send[to, i[0] * XC + c, spread, :] = held[0][(*i, rows, lanes(c))]
            else:
                send[to, 2 * XC + n - 1, spread, :] = held[n][(*i, rows, mine)].astype(jnp.float32)


MESSAGES = ((0, 1, 2), (3, 4), (5, 6), (7, 8))
OTHER = (1, 2, 3, 0)


def parcel_piece(recv):
    flat = recv.reshape(GROUP * PARCEL * 8, 128)
    return lambda y, n, row, par: flat[pl.ds((y * SPACE * PARCEL + n) * 8 + row * 2 + par, SPACE, stride=PARCEL * 8), :]


def unpack_shared_kernel(recv, label, force, low, high):
    piece = parcel_piece(recv)
    for y in range(Y):
        for row in range(ROWS):
            for par in range(2):
                for n, ref in enumerate((force, label)):
                    part = piece(y, 2 * XC + 1 + n, row, par)
                    ref[row, par, y] = part
                    if row < HALO:
                        low[n, row, par, y] = part
                    if row >= ROWS - HALO:
                        high[n, row - ROWS + HALO, par, y] = part


def unpack_kernel(recv, order, *messages):
    piece = parcel_piece(recv)
    for y in range(Y):
        for row in range(ROWS):
            for par in range(2):
                for tt in range(2):
                    for ref, starts in zip(messages, MESSAGES):
                        if 2 * y + tt + 1 in starts:
                            for c in range(XC):
                                ref[starts.index(2 * y + tt + 1), row, par, c] = piece(y, tt * XC + c, row, par)
                messages[0][0, row, par, y] = piece(y, 2 * XC, row, par)


def hold_kernel(source, order, out):
    out[...] = source[...]


def pack_parcels(n, ys, rows, back, scratch, done):
    flat = scratch.reshape(len(ys) * SPACE * 2 * XC * 8, 128)
    copies = []
    for m, y in enumerate(ys):
        for tt in range(2):
            for row in range(ROWS):
                for par, part in enumerate(rows(2 * y + tt, row)):
                    for c in range(XC):
                        at = (m * SPACE * 2 + tt) * XC + c
                        flat[pl.ds(at * 8 + row * 2 + par, SPACE, stride=2 * XC * 8), :] = part[c]
        to = back.at[pl.ds(y * SPACE, SPACE), pl.ds(n * 2 * XC, 2 * XC)]
        copies.append(pltpu.make_async_copy(scratch.at[pl.ds(m * SPACE, SPACE)], to, done.at[m]))
        copies[-1].start()
    for copy in copies:
        copy.wait()


def residual_pack_kernel(times, order, *refs):
    pack_parcels(1, range(Y), residual_rows(times, refs), *refs[-3:])


def early_pack_kernel(early, given, *refs):
    pack_parcels(0, range(Y // 2), lambda k, i: pair(early, k, i), *refs)


def finish_kernel(times, coef, start, below, above, *refs):
    back, errors, scratch, done = refs[-4:]
    advance(coef, residual_rows(times, refs), 4, 4, block(start, start.shape[0] - 1), below, above, errors)
    pack_parcels(0, range(Y // 2, Y), lambda k, i: pair(errors, k - 4, i), back, scratch, done)


def pack_call(kernel, alias, count, *args, more=()):
    return pl.pallas_call(
        kernel,
        out_shape=f32(GROUP, 4 * XC, 8, 128),
        in_specs=[VMEM] * (len(args) - alias) + [pl.BlockSpec(memory_space=pl.ANY)] * alias,
        out_specs=pl.BlockSpec(memory_space=pl.ANY),
        scratch_shapes=[*more, pltpu.VMEM((count * SPACE, 2 * XC, 8, 128), jnp.float32), pltpu.SemaphoreType.DMA((count,))],
        input_output_aliases={len(args) - 1: 0} if alias else {},
        compiler_params=pltpu.CompilerParams(vmem_limit_bytes=16 << 20),
        cost_estimate=pl.CostEstimate(flops=0, bytes_accessed=1024, transcendentals=0),
    )(*args)


def return_kernel(at_ref, recv, field, updated, residual, new, rest, done):
    copies = []
    for tt in range(2):
        for z in range(2):
            spread = pl.ds(z, ROWS, stride=2)
            for n in range(GROUP):
                rows = slice(ROWS * BLOCK_OF[n], ROWS * BLOCK_OF[n] + ROWS)
                j = mirrored(at_ref[0], n)
                for c in range(XC):
                    here = (tt, z, rows, lanes(c))
                    new[here] = field[here] + recv[j, tt * XC + c, spread, :]
                    rest[here] = recv[j, (2 + tt) * XC + c, spread, :]
            for held, out in ((new, updated), (rest, residual)):
                copies.append(pltpu.make_async_copy(held.at[tt, z], out.at[tt, z], done.at[len(copies)]))
                copies[-1].start()
    for copy in copies:
        copy.wait()


def coefficient_kernel(diffusion, drift, label, below, above, coef):
    lane = lax.broadcasted_iota(jnp.int32, (SPACE, 128), 1)
    tables = [jnp.zeros((SPACE, 128), jnp.float32)] * 8
    for n in range(diffusion.shape[0]):
        a = diffusion[n]
        bz, by, bx = a * drift[0, n], a * drift[1, n], a * drift[2, n]
        values = [1.0 - 6.0 * a, a - bz, a + bz, a - by, a + by, a - bx, a + bx, 1.0 - 6.0 * (a * COARSEN)]
        tables = [jnp.where(lane == n, value, table) for value, table in zip(values, tables)]
    for i in range(-HALO, ROWS + HALO):
        ref, at = (below, (1, HALO + i)) if i < 0 else (above, (1, i - ROWS)) if i >= ROWS else (label, (i,))
        for par in range(2):
            for c in range(XC):
                index = ref[(*at, par, c)].astype(jnp.int32)
                for t in range(8):
                    coef[t, HALO + i, par, c] = jnp.take_along_axis(tables[t], index, axis=1, mode="promise_in_bounds")


def x_shifts(v):
    lane = lax.broadcasted_iota(jnp.int32, v.shape, 2)
    before = pltpu.roll(v, 1, 2)
    after = pltpu.roll(v, 127, 2)
    before = jnp.where(lane == 0, jnp.concatenate([before[-1:], before[:-1]], 0), before)
    after = jnp.where(lane == 127, jnp.concatenate([after[1:], after[:1]], 0), after)
    return before, after


def sweep_row(coef, row, v, up, down, extra, coarse):
    at = HALO + row
    result = []
    for p in range(2):
        if p == 0:
            z_above, z_below = v[1], pltpu.roll(v[1], 1, 1)
        else:
            z_above, z_below = pltpu.roll(v[0], SPACE - 1, 1), v[0]
        before, after = x_shifts(v[p])
        total = coef[1, at, p] * z_above + coef[2, at, p] * z_below
        if up is not None:
            total = total + coef[3, at, p] * up[p]
        if down is not None:
            total = total + coef[4, at, p] * down[p]
        total = total + coef[5, at, p] * after + coef[6, at, p] * before
        if coarse:
            total = coef[7, at, p] * v[p] + COARSEN * total
        else:
            total = coef[0, at, p] * v[p] + total
        if extra is not None:
            total = total + extra[p]
        result.append(total)
    return result


def pair(ref, *at):
    return [ref[(*at, 0)], ref[(*at, 1)]]


def put(ref, at, value):
    for p in range(2):
        ref[(*at, p)] = value[p]


def fine_times(coef, force, starts):
    all_rows = []
    for own, below, above in starts:
        rows = {i: own(i) for i in range(ROWS)}
        rows |= {i - ROWS: below(i) for i in range(ROWS)}
        rows |= {i + ROWS: above(i) for i in range(ROWS)}
        all_rows.append(rows)
    for step in range(COARSEN):
        reach = COARSEN - 1 - step
        new = [{} for _ in starts]
        for i in range(-reach, ROWS + reach):
            for rows, out in zip(all_rows, new):
                out[i] = sweep_row(coef, i, rows[i], rows[i + 1], rows[i - 1], force(i), False)
        all_rows = new
    return [[rows[i] for i in range(ROWS)] for rows in all_rows]


def minus(a, b):
    return [x - y for x, y in zip(a, b)]


def fine_kernel(n, coef, force, edge_below, edge_above, starts, below, above, *refs):
    ks = MESSAGES[n]
    other, results = refs[0], refs[-1 - (8 in ks) :]

    def extra(i):
        return pair(edge_below, 0, i + HALO) if i < 0 else pair(edge_above, 0, i - ROWS) if i >= ROWS else pair(force, i)

    made = fine_times(
        coef, extra, [[lambda i, ref=ref, m=m: pair(ref, m, i) for ref in (starts, below, above)] for m in range(len(ks))]
    )
    for m, (k, rows) in enumerate(zip(ks, made)):
        for i in range(ROWS):
            if k == 8:
                put(results[1], (0, i), rows[i])
            else:
                ref, holder = (starts, ks) if k + 1 in ks else (other, MESSAGES[OTHER[n]])
                put(results[0], (m, i), minus(rows[i], pair(ref, holder.index(k + 1), i)))


def residual_rows(times, refs):
    def at(k, i):
        n = next(n for n, ks in enumerate(times) if k in ks)
        return pair(refs[n], times[n].index(k), i)

    return at


def trajectory(coef, r, first, width, start, low, high):
    rows = start
    for j in range(width):
        put(low, (j,), rows[0])
        put(high, (j,), rows[-1])
        if j + 1 < width:
            rows = [
                sweep_row(
                    coef, i, rows[i], rows[i + 1] if i + 1 < ROWS else None, rows[i - 1] if i else None,
                    r(first + j, i), True,
                )
                for i in range(ROWS)
            ]


def advance(coef, r, first, width, start, below, above, store):
    rows = start
    dev_low, dev_high = {}, {}
    for j in range(width):
        under, over = pair(below, j), pair(above, j)
        if 1 in dev_low:
            under = [a + b for a, b in zip(under, dev_low[1])]
            over = [a + b for a, b in zip(over, dev_high[1])]
        padded = [under] + rows + [over]
        new_low, new_high = {}, {}
        for i in range(1, min(j + 1, width - j - 1) + 1):
            source_low = rows[0] if i == 1 else dev_low[i - 1]
            source_high = rows[-1] if i == 1 else dev_high[i - 1]
            if i <= j:
                new_low[i] = sweep_row(coef, -i, dev_low[i], source_low, dev_low.get(i + 1), None, True)
                new_high[i] = sweep_row(coef, ROWS - 1 + i, dev_high[i], dev_high.get(i + 1), source_high, None, True)
            else:
                new_low[i] = [COARSEN * coef[3, HALO - i, p] * source_low[p] for p in range(2)]
                new_high[i] = [COARSEN * coef[4, HALO + ROWS - 1 + i, p] * source_high[p] for p in range(2)]
        rows = [sweep_row(coef, i, padded[i + 1], padded[i + 2], padded[i], r(first + j, i), True) for i in range(ROWS)]
        dev_low, dev_high = new_low, new_high
        if store is not None:
            for i in range(ROWS):
                put(store, (j, i), rows[i])
    return rows


def block(ref, *at):
    return [pair(ref, *at, i) for i in range(ROWS)]


def start_kernel(times, time, width, coef, start, *refs):
    low, high = refs[-2:]
    trajectory(coef, residual_rows(times, refs), time, width, block(start, 0), low, high)


def middle_kernel(times, time, width, then, whole, coef, start, below, above, *refs):
    errors, low, high = refs[-3:]
    r = residual_rows(times, refs)
    rows = advance(coef, r, time, width, block(start, 0), below, above, errors if whole else None)
    if not whole:
        for i in range(ROWS):
            put(errors, (0, i), rows[i])
    trajectory(coef, r, time + width, then, rows, low, high)


def end_kernel(times, coef, start, below, above, *refs):
    rows = advance(coef, residual_rows(times, refs), 4, 4, block(start, 0), below, above, None)
    for i in range(ROWS):
        put(refs[-1], (0, i), rows[i])


def exchange(low, high):
    return lax.ppermute(high, ALL, UP), lax.ppermute(low, ALL, DOWN)


def coarse(coef, r, start, time, behind, whole):
    a, b = 4 - time, 4
    r = list(r)

    def step(kernel, outs, flops, *args):
        times, arrays = [ks for ks, _ in r], [array for _, array in r]
        return call(functools.partial(kernel, times), outs, coef, *args, *arrays, flops=flops)

    low, high = step(lambda ks, *refs: start_kernel(ks, time, a, *refs), [f32(a, *ROW)] * 2, 500_000_000, start)
    below, above = exchange(low, high)
    r += behind[0](low)
    early, low, high = step(
        lambda ks, *refs: middle_kernel(ks, time, a, b, whole, *refs),
        [f32(a if whole else 1, ROWS, *ROW)] + [f32(b, *ROW)] * 2, 1_000_000_000, start, below, above,
    )
    below, above = exchange(low, high)
    r += behind[1](low, early)
    return early, below, above, r


def choose_kernel(at_ref, first, beyond, starts, out):
    @pl.when(at_ref[0] == 0)
    def _():
        out[0] = first[0]

    @pl.when(at_ref[0] == 1)
    def _():
        out[0] = beyond[0] - starts[1]


def shards(initial, c_values, forcing, classes, diffusion, drift):
    at = jnp.stack([lax.axis_index("xh"), lax.axis_index("y")])
    one = f32(ROWS, *ROW)

    inputs = (c_values, initial, forcing, classes)
    send = pl.pallas_call(
        pack_kernel,
        out_shape=f32(GROUP, PARCEL, 8, 128),
        in_specs=[SMEM] + [pl.BlockSpec(memory_space=pl.ANY)] * 4,
        out_specs=VMEM,
        scratch_shapes=[pltpu.VMEM(a.shape, a.dtype) for a in inputs] + [pltpu.SemaphoreType.DMA((10,))],
        compiler_params=pltpu.CompilerParams(vmem_limit_bytes=56 << 20),
    )(at, *inputs)
    recv = lax.all_to_all(send, RING, 0, 0, tiled=True)
    label, force, low, high = call(unpack_shared_kernel, [one, one] + [f32(2, HALO, *ROW)] * 2, recv)
    edges = exchange(low, high)
    starts = call(unpack_kernel, [f32(len(ks), ROWS, *ROW) for ks in MESSAGES], recv, low)
    halos = [exchange(message, message) for message in starts[:2]]
    coef = call(
        coefficient_kernel, f32(8, ROWS + 2 * HALO, *ROW), diffusion, drift, label, *edges, flops=3_000_000_000, scalars=2
    )

    def fine(n, halo, *order):
        ks = [k for k in MESSAGES[n] if k < 8]
        results = [f32(len(ks), ROWS, *ROW)] + [f32(1, ROWS, *ROW)] * (8 in MESSAGES[n])
        work = 1_500_000_000 * len(MESSAGES[n])
        kernel = functools.partial(fine_kernel, n)
        return call(kernel, results, coef, force, *edges, starts[n], *halo, starts[OTHER[n]], *order, flops=0)

    r = [(MESSAGES[0], fine(0, halos[0])[0])]
    third = call(hold_kernel, f32(*starts[2].shape), starts[2], coef)
    halos.append(exchange(third, third))
    made = []

    def first_behind(order):
        made.extend((MESSAGES[n], fine(n, halos[n], order)[0]) for n in (1, 2))
        held = call(hold_kernel, f32(*starts[3].shape), starts[3], order)
        halos.append(exchange(held, held))
        return made[:2]

    def second_behind(order, early):
        residual, beyond = fine(3, halos[3], order)
        made.extend([beyond, ((7,), residual)])
        return made[3:]

    *given, r_all = coarse(coef, r, r[0][1], 1, (first_behind, second_behind), False)
    kernel = functools.partial(end_kernel, [ks for ks, _ in r_all])
    last = call(kernel, f32(1, ROWS, *ROW), coef, *given, *[array for _, array in r_all], flops=0)
    beyond = lax.ppermute(made[2], ALL, ACROSS)
    start = lax.ppermute(last, ALL, ACROSS)
    first = call(choose_kernel, f32(1, ROWS, *ROW), at, r[0][1], beyond, starts[0], scalars=1)
    r = [((0,), first), r[0], *made[:2], made[3]]
    times, arrays = [ks for ks, _ in r], [array for _, array in r]
    back = []

    def pack_residual(order):
        back.append(pack_call(functools.partial(residual_pack_kernel, times), 0, Y, order, *arrays))
        return []

    def pack_early(order, early):
        back.append(pack_call(early_pack_kernel, 1, Y // 2, early, back[0]))
        return []

    *given, _ = coarse(coef, r, start, 0, (pack_residual, pack_early), True)
    errors = [pltpu.VMEM((4, ROWS, *ROW), jnp.float32)]
    kernel = functools.partial(finish_kernel, times)
    back = pack_call(kernel, 1, Y // 2, coef, *given, *arrays, back[1], more=errors)
    got = lax.all_to_all(back, RING, 0, 0, tiled=True)
    return tuple(
        pl.pallas_call(
            return_kernel,
            out_shape=[f32(*c_values.shape)] * 2,
            in_specs=[SMEM, VMEM, VMEM],
            out_specs=[pl.BlockSpec(memory_space=pl.ANY)] * 2,
            scratch_shapes=[pltpu.VMEM(c_values.shape, jnp.float32)] * 2 + [pltpu.SemaphoreType.DMA((8,))],
            compiler_params=pltpu.CompilerParams(vmem_limit_bytes=16 << 20),
        )(at, got, c_values)
    )


def solution(mesh):
    split = Mesh(np.asarray(mesh.devices).reshape(XH, Y, SPACE), ("xh", "y", "space"))
    return jax.shard_map(
        shards,
        mesh=split,
        in_specs=(P("space"), P(TM, "space"), P("space"), P("space"), P(), P()),
        out_specs=(P(TM, "space"), P(TM, "space")),
        check_vma=False,
    )
```
